32 devices in a mesh: groups: 2 (over y), dp: 4 (over z), tensor: 2 (over x), sub: 2 (over core).
Axes of the slice: x: 2, y: 2, z: 4, core: 2. Of those that a mesh axis runs over, the one named last changes fastest.
Arguments:
- hidden: bfloat16 [128, 32, 5120], P(('groups', 'dp'), None, ('tensor', 'sub')), parts along dimension 0, may hold values from -150 to 150
- seq_len: int32 [128], P(('groups', 'dp')), parts along dimension 0, may hold values from 1 to 32, as said below
- target_rank: int32 [128], P(('groups', 'dp')), parts along dimension 0, may hold values from 0 to 3, as said below
- in_gain: float32 [5120], replicated, may hold values from 0.25 to 1.75
- joined_projection_weight: bfloat16 [5120, 4, 1280], P('dp', 'tensor'), may hold values from -0.078125 to 0.078125
- query_gain: float32 [128], replicated, may hold values from 0.1 to 1.9
- k_gain: float32 [128], replicated, may hold values from 0.1 to 1.9
Outputs:
- key_cache: bfloat16 [128, 32, 512], P(('groups', 'dp'), 'sub', 'tensor'), parts along dimension 0
- value_cache: bfloat16 [128, 32, 512], P(('groups', 'dp'), 'sub', 'tensor'), parts along dimension 0
- context: bfloat16 [128, 32, 4, 1024], P(('groups', 'dp'), None, 'tensor', 'sub'), parts along dimension 0
The draws below stay inside these ranges and needn't reach their ends.
There are 2 independent parts, one for each index of `groups`. The reference program is written for one: setup_inputs(seed, part) draws one part's arguments, and reference() takes and returns one part's arrays. A program takes and returns all parts, laid end to end along the dimension named above; an argument that names none is the same for every part. Nothing has to cross between parts.
Inputs may be any that keep to these rules, and one draw needn't show every extreme that they name: `seq_len`: positions from a sequence's length on hold padding. `target_rank`: every dp rank receives exactly 16 sequences, at most 4 of them from any one dp rank.
All inputs are finite; a program needn't handle non-finite values.
Results may differ from the reference program's by a relative error of at most 0.0075.
Values may be sent and summed in bfloat16 or wider, within the bound.
A program may use at most 128 MiB of HBM per device.

```python
import jax
import jax.numpy as jnp
from jax import lax

MODEL_WIDTH = 5120
KV_HEAD_COUNT = 4
HEAD_SIZE = 128
QUERY_PER_KV = 8
SEQ_DEV = 16
TOKEN_SLOTS = 32
SEQUENCE_COUNT = 64


def shuffles(key, ranks):
    score = jax.random.randint(key, (ranks, SEQ_DEV), 0, 1 << 20) * SEQ_DEV
    score = score + jnp.arange(SEQ_DEV, dtype=jnp.int32)[None, :]
    return jnp.argsort(score, axis=1).astype(jnp.int32)


def draw_target_rank(key, part):
    key = jax.random.fold_in(key, 5)
    ranks = SEQUENCE_COUNT // SEQ_DEV
    relabel_key, shift_key, source_key = jax.random.split(key, 3)
    relabel = jax.random.permutation(relabel_key, ranks).astype(jnp.int32)
    inverse = jnp.argsort(relabel).astype(jnp.int32)
    rounds = (SEQ_DEV + ranks - 1) // ranks
    round_keys = jax.random.split(shift_key, rounds)
    shifts = jnp.concatenate([jax.random.permutation(round_keys[step], ranks) for step in range(rounds)])
    shifts = shifts[:SEQ_DEV].astype(jnp.int32)
    source_order = shuffles(source_key, ranks)
    target_label = (inverse[:, None] - shifts[source_order]) % ranks
    target_rank = relabel[target_label]
    return target_rank.reshape(SEQUENCE_COUNT).astype(jnp.int32)


def draw_seq_len(key, part):
    key = jax.random.fold_in(key, 7)
    base_key, top_key, low_key = jax.random.split(key, 3)
    lengths = jax.random.randint(base_key, (SEQUENCE_COUNT,), 1, TOKEN_SLOTS + 1)
    longest = jax.random.randint(top_key, (), 0, SEQUENCE_COUNT)
    shortest = (longest + jax.random.randint(low_key, (), 1, SEQUENCE_COUNT)) % SEQUENCE_COUNT
    lengths = lengths.at[longest].set(TOKEN_SLOTS).at[shortest].set(1)
    return lengths.astype(jnp.int32)


def draw_hidden(key, part):
    key = jax.random.fold_in(key, 11)
    base_key, row_key, column_key = jax.random.split(key, 3)
    base = jnp.clip(jax.random.normal(base_key, (SEQUENCE_COUNT, TOKEN_SLOTS, MODEL_WIDTH), jnp.float32), -4.0, 4.0)
    row_scale = jnp.exp(jax.random.uniform(row_key, (SEQUENCE_COUNT, TOKEN_SLOTS, 1), jnp.float32, 0.0, 2.3025851))
    column_scale = jnp.exp(jax.random.uniform(column_key, (1, 1, MODEL_WIDTH), jnp.float32, 0.0, 2.3025851))
    return (base * row_scale * column_scale / 3.0).astype(jnp.bfloat16)


def level_of(key, extent, shards, smallest, high):
    level = 1.0
    for position, blocks in shards:
        heights = jax.random.uniform(jax.random.fold_in(jax.random.fold_in(key, 6), position), (blocks,), jnp.float32, smallest / len(shards), high / len(shards))
        level = level * jnp.repeat(jnp.exp(heights), extent[position] // blocks).reshape((-1,) + (1,) * (len(extent) - 1 - position))
    return level


def centred(own_key, extent, width, limit, cuts=(), kind=jnp.bfloat16):
    result = width * jax.random.normal(own_key, extent, jnp.float32)
    if cuts:
        result = result * level_of(own_key, extent, cuts, -0.22, 0.18)
    return jnp.clip(result, -limit, limit).astype(kind)


def setup_inputs(seed: int = 0, part: int = 0) -> dict:
    keys = jax.random.split(jax.random.key(seed), 8)
    own_keys = jax.random.split(jax.random.fold_in(keys[7], part), 8)
    return {
        "hidden": draw_hidden(jax.random.fold_in(jax.random.fold_in(keys[7], part), 71), part),
        "seq_len": draw_seq_len(jax.random.fold_in(jax.random.fold_in(keys[7], part), 71), part),
        "target_rank": draw_target_rank(jax.random.fold_in(jax.random.fold_in(keys[7], part), 71), part),
        "in_gain": jnp.clip(1.0 + 0.15 * jax.random.normal(keys[3], (MODEL_WIDTH,), jnp.float32), 0.25, 1.75),
        "joined_projection_weight": centred(keys[4], (MODEL_WIDTH, KV_HEAD_COUNT, (QUERY_PER_KV + 2) * HEAD_SIZE), MODEL_WIDTH ** -0.5, 0.078125, ((0, 4), (1, 2))),
        "query_gain": jnp.clip(1.0 + 0.18 * jax.random.normal(keys[5], (HEAD_SIZE,), jnp.float32), 0.1, 1.9),
        "k_gain": jnp.clip(1.0 + 0.18 * jax.random.normal(keys[6], (HEAD_SIZE,), jnp.float32), 0.1, 1.9),
    }


EPS = 1e-06
THETA = 1000000.0

def per_head_norm(value_rows, gain):
    square_mean = lax.optimization_barrier(jnp.mean(value_rows * value_rows, axis=-1, keepdims=True))
    return value_rows * lax.rsqrt(square_mean + EPS) * gain.astype(jnp.float32)

def rotary_embed(value_rows, token_positions):
    half_width = value_rows.shape[-1] // 2
    frequency = THETA ** (-(2.0 * jnp.arange(half_width, dtype=jnp.float32)) / value_rows.shape[-1])
    angle = token_positions.astype(jnp.float32)[:, None] * frequency[None, :]
    cosine = jnp.cos(angle)[None, :, None, :]
    sine = jnp.sin(angle)[None, :, None, :]
    first = value_rows[..., :half_width]
    second = value_rows[..., half_width:]
    return jnp.concatenate([first * cosine - second * sine, second * cosine + first * sine], axis=-1)

def reference(hidden, seq_len, target_rank, in_gain, joined_projection_weight, query_gain, k_gain):
    order_ids = jnp.arange(SEQUENCE_COUNT, dtype=jnp.int32)
    same_target = (target_rank[:, None] == target_rank[None, :]) & (order_ids[None, :] < order_ids[:, None])
    earlier = lax.optimization_barrier(jnp.sum(same_target.astype(jnp.int32), axis=1)).astype(jnp.int32)
    target_index = (target_rank * SEQ_DEV + earlier).astype(jnp.int32)
    moved = jnp.zeros_like(hidden).at[target_index].set(hidden)
    lengths = jnp.zeros_like(seq_len).at[target_index].set(seq_len)
    tokens = moved.reshape(SEQUENCE_COUNT * TOKEN_SLOTS, MODEL_WIDTH).astype(jnp.float32)
    square_mean = lax.optimization_barrier(jnp.mean(tokens * tokens, axis=-1, keepdims=True))
    normed_query = (tokens * lax.rsqrt(square_mean + EPS) * in_gain.astype(jnp.float32)).astype(jnp.bfloat16)
    mixed_projection = jnp.dot(normed_query, joined_projection_weight.reshape(MODEL_WIDTH, KV_HEAD_COUNT * (QUERY_PER_KV + 2) * HEAD_SIZE), preferred_element_type=jnp.float32)
    mixed_projection = mixed_projection.reshape(SEQUENCE_COUNT, TOKEN_SLOTS, KV_HEAD_COUNT, QUERY_PER_KV + 2, HEAD_SIZE)
    token_positions = jnp.arange(TOKEN_SLOTS, dtype=jnp.int32)
    live = token_positions[None, :] < lengths[:, None]
    query_rows = rotary_embed(per_head_norm(mixed_projection[:, :, :, :QUERY_PER_KV, :].reshape(SEQUENCE_COUNT, TOKEN_SLOTS, KV_HEAD_COUNT * QUERY_PER_KV, HEAD_SIZE), query_gain), token_positions)
    query_rows = query_rows.astype(jnp.bfloat16)
    key_rows = rotary_embed(per_head_norm(mixed_projection[:, :, :, QUERY_PER_KV, :], k_gain), token_positions)
    key_rows = jnp.where(live[:, :, None, None], key_rows, 0.0).astype(jnp.bfloat16)
    value_rows = jnp.where(live[:, :, None, None], mixed_projection[:, :, :, QUERY_PER_KV + 1, :], 0.0).astype(jnp.bfloat16)
    grouped_heads = query_rows.astype(jnp.float32).reshape(SEQUENCE_COUNT, TOKEN_SLOTS, KV_HEAD_COUNT, QUERY_PER_KV, HEAD_SIZE)
    scores = jnp.einsum('nqghd,nkgd->nghqk', grouped_heads, key_rows.astype(jnp.float32)) * HEAD_SIZE ** (-0.5)
    causal = token_positions[None, :] <= token_positions[:, None]
    allowed = causal[None, None, None, :, :] & live[:, None, None, None, :]
    weights = jnp.where(allowed, jnp.exp(scores), 0.0)
    probs = (weights / lax.optimization_barrier(jnp.sum(weights, axis=-1, keepdims=True))).astype(jnp.bfloat16)
    context = jnp.einsum('nghqk,nkgd->nqghd', probs.astype(jnp.float32), value_rows.astype(jnp.float32))
    context = jnp.where(live[:, :, None, None, None], context, 0.0)
    context = context.reshape(SEQUENCE_COUNT, TOKEN_SLOTS, KV_HEAD_COUNT, QUERY_PER_KV * HEAD_SIZE).astype(jnp.bfloat16)
    return (key_rows.reshape(SEQUENCE_COUNT, TOKEN_SLOTS, KV_HEAD_COUNT * HEAD_SIZE), value_rows.reshape(SEQUENCE_COUNT, TOKEN_SLOTS, KV_HEAD_COUNT * HEAD_SIZE), context)
```

```python
import jax
import jax.numpy as jnp
from jax import lax
from jax.sharding import PartitionSpec as P

EPS = 1e-06
THETA = 1000000.0


def per_head_norm(value_rows, gain):
    square_mean = jnp.mean(value_rows * value_rows, axis=-1, keepdims=True)
    return value_rows * lax.rsqrt(square_mean + EPS) * gain


def rotary_embed(value_rows, token_positions):
    half_width = value_rows.shape[-1] // 2
    frequency = THETA ** (-(2.0 * jnp.arange(half_width, dtype=jnp.float32)) / value_rows.shape[-1])
    angle = token_positions.astype(jnp.float32)[:, None] * frequency[None, :]
    cosine = jnp.cos(angle)[None, :, None, :]
    sine = jnp.sin(angle)[None, :, None, :]
    first = value_rows[..., :half_width]
    second = value_rows[..., half_width:]
    return jnp.concatenate(
        [first * cosine - second * sine, second * cosine + first * sine], axis=-1
    )


def body(hidden, seq_len, target_rank, in_gain, joined_projection_weight, query_gain, k_gain):
    slots, length, width = hidden.shape
    ranks = lax.axis_size("dp")
    pair = -(-slots // ranks)
    lanes = ranks * pair
    local = jnp.arange(slots, dtype=jnp.int32)
    same_target = (target_rank[:, None] == target_rank[None, :]) & (local[None, :] < local[:, None])
    earlier = jnp.sum(same_target.astype(jnp.int32), axis=1)
    position = target_rank * pair + earlier
    lane_ids = jnp.arange(lanes, dtype=jnp.int32)
    hits = lane_ids[:, None] == position[None, :]
    filled = jnp.any(hits, axis=1)
    source = jnp.sum(jnp.where(hits, local[None, :], 0), axis=1)
    outgoing = jnp.where(
        filled[:, None, None], jnp.take(hidden, source, axis=0), jnp.zeros((), hidden.dtype)
    )
    sent_length = jnp.where(filled, jnp.take(seq_len, source), 0)
    arrived, arrived_length = (
        lax.all_to_all(
            outgoing.reshape(ranks, pair, length, width),
            "dp",
            split_axis=0,
            concat_axis=0,
            tiled=True,
        ),
        lax.all_to_all(
            sent_length.reshape(ranks, pair), "dp", split_axis=0, concat_axis=0, tiled=True
        ),
    )
    arrived = arrived.reshape(lanes, length, width)
    arrived_length = arrived_length.reshape(lanes)
    present = arrived_length > 0
    arrived_slot = jnp.cumsum(present.astype(jnp.int32)) - 1
    matches = (arrived_slot[None, :] == local[:, None]) & present[None, :]
    chosen = jnp.sum(jnp.where(matches, lane_ids[None, :], 0), axis=1)
    lengths = jnp.sum(jnp.where(matches, arrived_length[None, :], 0), axis=1)
    moved = arrived if lanes == slots else jnp.take(arrived, chosen, axis=0)
    whole = lax.all_gather(moved, ("tensor", "sub"), axis=2, tiled=True)
    tokens = whole.reshape(slots * length, whole.shape[2]).astype(jnp.float32)
    square_mean = jnp.mean(tokens * tokens, axis=-1, keepdims=True)
    normed_query = (tokens * lax.rsqrt(square_mean + EPS) * in_gain).astype(jnp.bfloat16)
    groups = joined_projection_weight.shape[1]
    head_dim = query_gain.shape[0]
    group_query = joined_projection_weight.shape[2] - 2 * head_dim
    half_heads = group_query // head_dim // lax.axis_size("sub")
    query_cols = half_heads * head_dim
    core = lax.axis_index("sub")
    own_query = lax.dynamic_slice_in_dim(joined_projection_weight, core * query_cols, query_cols, 2)
    extra = joined_projection_weight[:, :, group_query:]
    columns = jnp.concatenate([own_query, extra], axis=2)
    span = columns.shape[2]
    flat_columns = columns.reshape(columns.shape[0], groups * span)
    copies = lax.axis_size("groups")
    rows = flat_columns.shape[0] // copies
    own_rows = lax.dynamic_slice_in_dim(flat_columns, lax.axis_index("groups") * rows, rows, 0)
    mixed_projection = jnp.dot(
        normed_query,
        lax.all_gather(own_rows, ("dp", "groups"), axis=0, tiled=True),
        preferred_element_type=jnp.float32,
    )
    mixed_projection = mixed_projection.reshape(slots, length, groups, span)
    token_positions = jnp.arange(length, dtype=jnp.int32)
    live = token_positions[None, :] < lengths[:, None]
    query_rows = mixed_projection[..., :query_cols].reshape(
        slots, length, groups * half_heads, head_dim
    )
    query_rows = rotary_embed(per_head_norm(query_rows, query_gain), token_positions).astype(
        jnp.bfloat16
    )
    key_rows = rotary_embed(
        per_head_norm(mixed_projection[..., query_cols : query_cols + head_dim], k_gain),
        token_positions,
    )
    key_rows = jnp.where(live[:, :, None, None], key_rows, 0.0).astype(jnp.bfloat16)
    value_rows = jnp.where(
        live[:, :, None, None], mixed_projection[..., query_cols + head_dim :], 0.0
    ).astype(jnp.bfloat16)
    grouped_heads = query_rows.reshape(slots, length, groups, half_heads, head_dim)
    scores = jnp.einsum(
        "nqghd,nkgd->nghqk", grouped_heads, key_rows, preferred_element_type=jnp.float32
    ) * head_dim ** (-0.5)
    causal = token_positions[None, :] <= token_positions[:, None]
    allowed = causal[None, None, None, :, :] & live[:, None, None, None, :]
    weights = jnp.where(allowed, jnp.exp(scores), 0.0)
    probs = (weights / jnp.sum(weights, axis=-1, keepdims=True)).astype(jnp.bfloat16)
    context = jnp.einsum("nghqk,nkgd->nqghd", probs, value_rows, preferred_element_type=jnp.float32)
    context = jnp.where(live[:, :, None, None, None], context, 0.0)
    context = context.reshape(slots, length, groups, half_heads * head_dim).astype(jnp.bfloat16)
    share = length // lax.axis_size("sub")
    key_share = lax.dynamic_slice_in_dim(key_rows, core * share, share, 1).reshape(
        slots, share, groups * head_dim
    )
    value_share = lax.dynamic_slice_in_dim(value_rows, core * share, share, 1).reshape(
        slots, share, groups * head_dim
    )
    return (key_share, value_share, context)


def solution(mesh):
    placed = (
        P(("groups", "dp"), None, ("tensor", "sub")),
        P(("groups", "dp")),
        P(("groups", "dp")),
        P(),
        P("dp", "tensor", None),
        P(),
        P(),
    )
    return jax.shard_map(
        body,
        mesh=mesh,
        in_specs=placed,
        out_specs=(
            P(("groups", "dp"), "sub", "tensor"),
            P(("groups", "dp"), "sub", "tensor"),
            P(("groups", "dp"), None, "tensor", "sub"),
        ),
        check_vma=False,
    )
```

```python
import functools

import jax
import jax.numpy as jnp
from jax import lax
from jax.experimental import pallas as pl
from jax.experimental.pallas import tpu as pltpu
from jax.sharding import PartitionSpec as P

EPS = 1e-06
THETA = 1000000.0


def per_head_norm(value_rows, gain):
    square_mean = jnp.mean(value_rows * value_rows, axis=-1, keepdims=True)
    return value_rows * lax.rsqrt(square_mean + EPS) * gain


def rotary_embed(value_rows, token_positions):
    half_width = value_rows.shape[-1] // 2
    frequency = THETA ** (-(2.0 * jnp.arange(half_width, dtype=jnp.float32)) / value_rows.shape[-1])
    angle = token_positions.astype(jnp.float32)[:, None] * frequency[None, :]
    cosine = jnp.cos(angle)[None, :, None, :]
    sine = jnp.sin(angle)[None, :, None, :]
    first = value_rows[..., :half_width]
    second = value_rows[..., half_width:]
    return jnp.concatenate(
        [first * cosine - second * sine, second * cosine + first * sine], axis=-1
    )


def body(hidden, seq_len, target_rank, in_gain, joined_projection_weight, query_gain, k_gain):
    slots, length, width = hidden.shape
    ranks = lax.axis_size("dp")
    pair = -(-slots // ranks)
    lanes = ranks * pair
    local = jnp.arange(slots, dtype=jnp.int32)
    same_target = (target_rank[:, None] == target_rank[None, :]) & (local[None, :] < local[:, None])
    earlier = jnp.sum(same_target.astype(jnp.int32), axis=1)
    position = target_rank * pair + earlier
    lane_ids = jnp.arange(lanes, dtype=jnp.int32)
    hits = lane_ids[:, None] == position[None, :]
    filled = jnp.any(hits, axis=1)
    source = jnp.sum(jnp.where(hits, local[None, :], 0), axis=1)
    outgoing = jnp.where(
        filled[:, None, None], jnp.take(hidden, source, axis=0), jnp.zeros((), hidden.dtype)
    )
    sent_length = jnp.where(filled, jnp.take(seq_len, source), 0)
    arrived, arrived_length = (
        lax.all_to_all(
            outgoing.reshape(ranks, pair, length, width),
            "dp",
            split_axis=0,
            concat_axis=0,
            tiled=True,
        ),
        lax.all_to_all(
            sent_length.reshape(ranks, pair), "dp", split_axis=0, concat_axis=0, tiled=True
        ),
    )
    arrived = arrived.reshape(lanes, length, width)
    arrived_length = arrived_length.reshape(lanes)
    present = arrived_length > 0
    arrived_slot = jnp.cumsum(present.astype(jnp.int32)) - 1
    matches = (arrived_slot[None, :] == local[:, None]) & present[None, :]
    chosen = jnp.sum(jnp.where(matches, lane_ids[None, :], 0), axis=1)
    lengths = jnp.sum(jnp.where(matches, arrived_length[None, :], 0), axis=1)
    moved = arrived if lanes == slots else jnp.take(arrived, chosen, axis=0)
    whole = lax.all_gather(moved, ("tensor", "sub"), axis=2, tiled=True)
    tokens = whole.reshape(slots * length, whole.shape[2]).astype(jnp.float32)
    square_mean = jnp.mean(tokens * tokens, axis=-1, keepdims=True)
    normed_query = (tokens * lax.rsqrt(square_mean + EPS) * in_gain).astype(jnp.bfloat16)
    groups = joined_projection_weight.shape[1]
    head_dim = query_gain.shape[0]
    group_query = joined_projection_weight.shape[2] - 2 * head_dim
    half_heads = group_query // head_dim // lax.axis_size("sub")
    query_cols = half_heads * head_dim
    core = lax.axis_index("sub")
    own_query = lax.dynamic_slice_in_dim(joined_projection_weight, core * query_cols, query_cols, 2)
    extra = joined_projection_weight[:, :, group_query:]
    columns = jnp.concatenate([own_query, extra], axis=2)
    span = columns.shape[2]
    flat_columns = columns.reshape(columns.shape[0], groups * span)
    copies = lax.axis_size("groups")
    rows = flat_columns.shape[0] // copies
    own_rows = lax.dynamic_slice_in_dim(flat_columns, lax.axis_index("groups") * rows, rows, 0)
    mixed_projection = jnp.dot(
        normed_query,
        lax.all_gather(own_rows, ("dp", "groups"), axis=0, tiled=True),
        preferred_element_type=jnp.float32,
    )
    mixed_projection = mixed_projection.reshape(slots, length, groups, span)
    token_positions = jnp.arange(length, dtype=jnp.int32)
    live = token_positions[None, :] < lengths[:, None]
    query_rows = mixed_projection[..., :query_cols].reshape(
        slots, length, groups * half_heads, head_dim
    )
    query_rows = rotary_embed(per_head_norm(query_rows, query_gain), token_positions).astype(
        jnp.bfloat16
    )
    key_rows = rotary_embed(
        per_head_norm(mixed_projection[..., query_cols : query_cols + head_dim], k_gain),
        token_positions,
    )
    key_rows = jnp.where(live[:, :, None, None], key_rows, 0.0).astype(jnp.bfloat16)
    value_rows = jnp.where(
        live[:, :, None, None], mixed_projection[..., query_cols + head_dim :], 0.0
    ).astype(jnp.bfloat16)
    grouped_heads = query_rows.reshape(slots, length, groups, half_heads, head_dim)
    scores = jnp.einsum(
        "nqghd,nkgd->nghqk", grouped_heads, key_rows, preferred_element_type=jnp.float32
    ) * head_dim ** (-0.5)
    causal = token_positions[None, :] <= token_positions[:, None]
    allowed = causal[None, None, None, :, :] & live[:, None, None, None, :]
    weights = jnp.where(allowed, jnp.exp(scores), 0.0)
    probs = (weights / jnp.sum(weights, axis=-1, keepdims=True)).astype(jnp.bfloat16)
    context = jnp.einsum("nghqk,nkgd->nqghd", probs, value_rows, preferred_element_type=jnp.float32)
    context = jnp.where(live[:, :, None, None, None], context, 0.0)
    context = context.reshape(slots, length, groups, half_heads * head_dim).astype(jnp.bfloat16)
    share = length // lax.axis_size("sub")
    key_share = lax.dynamic_slice_in_dim(key_rows, core * share, share, 1).reshape(
        slots, share, groups * head_dim
    )
    value_share = lax.dynamic_slice_in_dim(value_rows, core * share, share, 1).reshape(
        slots, share, groups * head_dim
    )
    return (key_share, value_share, context)


CHUNK = 256


def exchange_kernel(
    tok, lens, w, q_out, kv_out, len_out,
    a, wm, psend, prec, own, ssend, srecv, kvown, kvrecv, lrecv,
    s1s, s1r, s2s, s2r, s3s, s3r, s4s, s4r,
    ws, wr, wfs, wfr, ps, pr, ss, sr, ls, lr, kvs, kvr,
):
    g = lax.axis_index("groups")
    z = lax.axis_index("dp")
    x = lax.axis_index("tensor")
    s = lax.axis_index("sub")
    here = z % 2
    pair = z // 2
    half = w.shape[1] // 2
    n_chunks = w.shape[0]
    x_mate = (g, z, 1 - x, s)
    sibling = (g, z, x, 1 - s)
    z_mate = (g, pair * 2 + (1 - here), x, s)
    y_mate = (1 - g, z, x, s)
    far = (g, (1 - pair) * 2 + here, x, s)

    barrier = pltpu.get_barrier_semaphore()
    for dz in range(1, 4):
        for dx in range(2):
            pl.semaphore_signal(
                barrier, inc=1, device_id=(g, (z + dz) % 4, (x + dx) % 2, s),
                device_id_type=pl.DeviceIdType.MESH,
            )
    for other in (x_mate, sibling, y_mate):
        pl.semaphore_signal(barrier, inc=1, device_id=other, device_id_type=pl.DeviceIdType.MESH)
    pl.semaphore_wait(barrier, 9)

    def remote(src, dst, send, recv, device):
        return pltpu.make_async_remote_copy(
            src_ref=src, dst_ref=dst, send_sem=send, recv_sem=recv,
            device_id=device, device_id_type=pl.DeviceIdType.MESH,
        )

    def first(o, b, h):
        target = 2 * ((x + 1 + o) % 2) + b
        src = tok.at[target, h]
        dst = a.at[o, s, z, h]
        zt = 2 * x + b
        stays = (zt == z) & (x == h)
        return (
            stays,
            remote(src, dst, s1s.at[o, b, h], s1r.at[o, z], (g, zt, h, s)),
            pltpu.make_async_copy(src, dst, s1r.at[o, z]),
        )

    def start_first(o):
        for b in range(2):
            for h in range(2):
                stays, away, local = first(o, b, h)
                pl.when(jnp.logical_not(stays))(away.start)
                pl.when(stays)(local.start)

    def arrived(o, zs):
        dst = a.at[o, s, zs, x]
        local = (pair == x) & (z == zs)
        pl.when(jnp.logical_not(local))(
            remote(dst, dst, s1s.at[o, 0, 0], s1r.at[o, zs], x_mate).wait_recv
        )
        pl.when(local)(pltpu.make_async_copy(tok.at[0, 0], dst, s1r.at[o, zs]).wait)

    def to_x(o, zs):
        piece = a.at[o, s, zs, x]
        return remote(piece, piece, s2s.at[o, zs], s2r.at[o, zs], x_mate)

    def from_x(o, zs):
        piece = a.at[o, s, zs, 1 - x]
        return remote(piece, piece, s2s.at[o, zs], s2r.at[o, zs], x_mate)

    def to_sub(o, zs):
        piece = a.at[o, s, zs, x]
        return remote(piece, piece, s3s.at[o, zs], s3r.at[o, zs], sibling)

    def from_sub(o, zs):
        piece = a.at[o, 1 - s, zs, x]
        return remote(piece, piece, s3s.at[o, zs], s3r.at[o, zs], sibling)

    def to_sub_late(o, zs):
        piece = a.at[o, s, zs, 1 - x]
        return remote(piece, piece, s4s.at[o, zs], s4r.at[o, zs], sibling)

    def from_sub_late(o, zs):
        piece = a.at[o, 1 - s, zs, 1 - x]
        return remote(piece, piece, s4s.at[o, zs], s4r.at[o, zs], sibling)

    def forward(o):
        for zs in range(4):
            arrived(o, zs)
            to_x(o, zs).start()
            to_sub(o, zs).start()
        for zs in range(4):
            from_x(o, zs).wait_recv()
            to_sub_late(o, zs).start()
        for zs in range(4):
            from_sub(o, zs).wait_recv()
            from_sub_late(o, zs).wait_recv()

    def w_copy(c):
        rows = pl.ds(pl.multiple_of(g * half, half), half)
        return remote(w.at[c, rows], wm.at[c, rows], ws.at[c], wr.at[c], z_mate)

    def w_forward(c):
        rows = pl.ds(pl.multiple_of(g * half, half), half)
        return remote(wm.at[c, rows], wm.at[c, rows], wfs.at[c], wfr.at[c], y_mate)

    def w_forwarded(c):
        rows = pl.ds(pl.multiple_of((1 - g) * half, half), half)
        return remote(wm.at[c, rows], wm.at[c, rows], wfs.at[c], wfr.at[c], y_mate)

    def p_copy(c):
        return remote(psend.at[c], prec.at[c], ps.at[c], pr.at[c], far)

    def s_copy():
        return remote(ssend, srecv, ss.at[0], sr.at[0], far)

    def kv_copy():
        return remote(kvown, kvrecv, kvs.at[0], kvr.at[0], sibling)

    def len_copy(step):
        zt = (z + step) % 4
        return remote(lens.at[zt], lrecv.at[z], ls.at[step], lr.at[step], (g, zt, x, s))

    def product(o, c):
        def tokens(block):
            t = a[o, block]
            return t.reshape(t.shape[0] * t.shape[1] * t.shape[2], t.shape[3])

        return jnp.dot(
            tokens(here), w[c], preferred_element_type=jnp.float32
        ) + jnp.dot(tokens(1 - here), wm[c], preferred_element_type=jnp.float32)

    def squares(o, zs, h):
        total = None
        for block in range(2):
            t = a[o, block, zs, h].astype(jnp.float32)
            part = jnp.sum(t * t, axis=1, keepdims=True)
            total = part if total is None else total + part
        return total

    start_first(0)
    for step in range(1, 4):
        len_copy(step).start()
    for c in range(n_chunks):
        w_copy(c).start()
    start_first(1)

    forward(0)

    piece_rows = a.shape[4]

    @pl.loop(0, 8)
    def _(i):
        rows = pl.ds(pl.multiple_of(i * piece_rows, piece_rows), piece_rows)
        ssend[rows, :] = jnp.broadcast_to(squares(0, i // 2, i % 2), (piece_rows, 128))

    s_copy().start()

    w_copy(0).wait_recv()
    w_forward(0).start()

    def send_partial(c):
        w_forwarded(c).wait_recv()
        psend[c] = product(0, c).astype(psend.dtype)
        p_copy(c).start()

    @pl.loop(1, n_chunks)
    def _(c):
        w_copy(c).wait_recv()
        w_forward(c).start()
        send_partial(c - 1)

    send_partial(n_chunks - 1)

    forward(1)

    @pl.loop(0, n_chunks)
    def _(c):
        own[c] = product(1, c)

    s_copy().wait_recv()

    @pl.loop(0, 8)
    def _(i):
        rows = pl.ds(pl.multiple_of(i * piece_rows, piece_rows), piece_rows)
        total = squares(1, i // 2, i % 2) + srecv[rows, :]
        srecv[rows, :] = lax.rsqrt(total / (4 * a.shape[5]) + EPS)

    scale = jnp.concatenate([srecv[...]] * (CHUNK // 128), axis=1)
    p_copy(0).wait_recv()
    kvown[...] = (own[0] + prec[0].astype(jnp.float32)) * scale
    kv_copy().start()
    kv_out[s] = kvown[...]

    @pl.loop(1, n_chunks)
    def _(c):
        p_copy(c).wait_recv()
        wide = jnp.concatenate([srecv[...]] * (CHUNK // 128), axis=1)
        q_out[c - 1] = (own[c] + prec[c].astype(jnp.float32)) * wide

    len_out[z] = lens[z]
    for step in range(1, 4):
        source = (z + 4 - step) % 4
        remote(lrecv.at[source], lrecv.at[source], ls.at[step], lr.at[step], x_mate).wait_recv()
        len_out[source] = lrecv[source]

    kv_copy().wait_recv()
    kv_out[1 - s] = kvrecv[...]

    for o in range(2):
        for b in range(2):
            for h in range(2):
                stays, away, _ = first(o, b, h)
                pl.when(jnp.logical_not(stays))(away.wait_send)
        for zs in range(4):
            to_x(o, zs).wait_send()
            to_sub(o, zs).wait_send()
            to_sub_late(o, zs).wait_send()
    for c in range(n_chunks):
        w_copy(c).wait_send()
        w_forward(c).wait_send()
        p_copy(c).wait_send()
    s_copy().wait_send()
    kv_copy().wait_send()
    for step in range(1, 4):
        len_copy(step).wait_send()


def exchange(tok, lens, w):
    chunks, width, columns = w.shape
    tokens = tok.shape[0] * tok.shape[1] * tok.shape[2]
    dma = pltpu.SemaphoreType.DMA
    vmem = pl.BlockSpec(memory_space=pltpu.VMEM)
    f32 = jnp.float32
    bf16 = jnp.bfloat16
    return pl.pallas_call(
        exchange_kernel,
        out_shape=(
            jax.ShapeDtypeStruct((chunks - 1, tokens, columns), f32),
            jax.ShapeDtypeStruct((2, tokens, columns), f32),
            jax.ShapeDtypeStruct(lens.shape, f32),
        ),
        in_specs=[pl.BlockSpec(memory_space=pl.ANY), vmem, vmem],
        out_specs=(vmem, vmem, vmem),
        scratch_shapes=[
            pltpu.VMEM((2, 2, 4, 2, tok.shape[2], width), bf16),
            pltpu.VMEM((chunks, width, columns), bf16),
            pltpu.VMEM((chunks, tokens, columns), bf16),
            pltpu.VMEM((chunks, tokens, columns), bf16),
            pltpu.VMEM((chunks, tokens, columns), f32),
            pltpu.VMEM((tokens, 128), f32),
            pltpu.VMEM((tokens, 128), f32),
            pltpu.VMEM((tokens, columns), f32),
            pltpu.VMEM((tokens, columns), f32),
            pltpu.VMEM(lens.shape, f32),
            dma((2, 2, 2)), dma((2, 4)), dma((2, 4)), dma((2, 4)),
            dma((2, 4)), dma((2, 4)), dma((2, 4)), dma((2, 4)),
            dma((chunks,)), dma((chunks,)), dma((chunks,)), dma((chunks,)),
            dma((chunks,)), dma((chunks,)), dma((1,)), dma((1,)),
            dma((4,)), dma((4,)), dma((1,)), dma((1,)),
        ],
        compiler_params=pltpu.CompilerParams(
            collective_id=0, has_side_effects=True, vmem_limit_bytes=48 << 20
        ),
        cost_estimate=pl.CostEstimate(
            flops=8 * tokens * width * chunks * columns, bytes_accessed=1 << 24, transcendentals=0
        ),
        name="exchange",
    )(tok, lens, w)


def attend_kernel(q_ref, kv_ref, len_ref, cos_ref, sin_ref, qg_ref, kg_ref, k_out, v_out, ctx_out):
    head = cos_ref.shape[1]
    rows = cos_ref.shape[0]
    seqs, share, _ = k_out.shape
    length = rows // seqs
    core = lax.axis_index("sub")
    len_key = jnp.broadcast_to(len_ref[0, 0:1, :], (rows, rows))
    len_query = len_key.T
    row_ids = lax.broadcasted_iota(jnp.int32, (rows, rows), 0)
    col_ids = lax.broadcasted_iota(jnp.int32, (rows, rows), 1)
    key_pos = (col_ids % length).astype(jnp.float32)
    query_pos = (row_ids % length).astype(jnp.float32)
    allowed = (
        (row_ids // length == col_ids // length) & (col_ids <= row_ids) & (key_pos < len_key)
    )
    live = query_pos < len_query
    cos = cos_ref[...]
    sin = sin_ref[...]

    def norm_rope(t, gain):
        mean = jnp.mean(t * t, axis=-1, keepdims=True)
        t = t * lax.rsqrt(mean + EPS) * gain
        return t * cos + pltpu.roll(t, head // 2, 1) * sin

    def part(t):
        t = t.reshape(seqs, length, head)
        return jnp.where(core == 0, t[:, :share], t[:, share:])

    kgain = kg_ref[...]
    qgain = qg_ref[...]
    n_groups = kv_ref.shape[2] // head
    heads = q_ref.shape[0] * q_ref.shape[2] // head // n_groups
    per_chunk = q_ref.shape[2] // head
    for group in range(n_groups):
        cols = slice(group * head, (group + 1) * head)
        key = jnp.where(live, norm_rope(kv_ref[0, :, cols], kgain), 0.0)
        value = jnp.where(live, kv_ref[1, :, cols], 0.0)
        k_out[:, :, cols] = part(key).astype(k_out.dtype)
        v_out[:, :, cols] = part(value).astype(v_out.dtype)
        key = key.astype(jnp.bfloat16)
        value = value.astype(jnp.bfloat16)
        for h in range(heads):
            n = group * heads + h
            at = n % per_chunk * head
            query = norm_rope(q_ref[n // per_chunk, :, at : at + head], qgain)
            scores = lax.dot_general(
                query.astype(jnp.bfloat16), key, (((1,), (1,)), ((), ())),
                preferred_element_type=jnp.float32,
            ) * head ** (-0.5)
            weights = jnp.where(allowed, jnp.exp(scores), 0.0)
            probs = weights / jnp.sum(weights, axis=-1, keepdims=True)
            out = jnp.dot(probs.astype(jnp.bfloat16), value, preferred_element_type=jnp.float32)
            ctx_out[:, n * head : (n + 1) * head] = jnp.where(live, out, 0.0).astype(ctx_out.dtype)


def attend(q, kv, lens, query_gain, k_gain, length, share):
    head = query_gain.shape[0]
    chunks, tokens, columns = q.shape
    blocks = lens.shape[0]
    rows = tokens // blocks
    seqs = rows // length
    frequency = THETA ** (-(2.0 * jnp.arange(head // 2, dtype=jnp.float32)) / head)
    positions = jnp.arange(rows, dtype=jnp.int32) % length
    angle = positions.astype(jnp.float32)[:, None] * frequency[None, :]
    cos = jnp.cos(angle)
    sin = jnp.sin(angle)
    whole = lambda *shape: pl.BlockSpec(shape, lambda i: (0,) * len(shape))
    cache = jax.ShapeDtypeStruct((tokens // length, share, columns), jnp.bfloat16)
    return pl.pallas_call(
        attend_kernel,
        grid=(blocks,),
        out_shape=(cache, cache, jax.ShapeDtypeStruct((tokens, chunks * columns), jnp.bfloat16)),
        in_specs=[
            pl.BlockSpec((chunks, rows, columns), lambda i: (0, i, 0)),
            pl.BlockSpec((2, rows, columns), lambda i: (0, i, 0)),
            pl.BlockSpec((1,) + lens.shape[1:], lambda i: (i, 0, 0)),
            whole(rows, head), whole(rows, head), whole(1, head), whole(1, head),
        ],
        out_specs=(
            pl.BlockSpec((seqs, share, columns), lambda i: (i, 0, 0)),
            pl.BlockSpec((seqs, share, columns), lambda i: (i, 0, 0)),
            pl.BlockSpec((rows, chunks * columns), lambda i: (i, 0)),
        ),
        compiler_params=pltpu.CompilerParams(vmem_limit_bytes=32 << 20),
        name="attend",
    )(
        q, kv, lens,
        jnp.concatenate([cos, cos], axis=1), jnp.concatenate([-sin, sin], axis=1),
        query_gain[None, :], k_gain[None, :],
    )


def paired_body(
    hidden, seq_len, target_rank, in_gain, joined_projection_weight, query_gain, k_gain
):
    slots, length, width = hidden.shape
    ranks = lax.axis_size("dp")
    pair = slots // ranks
    local = jnp.arange(slots, dtype=jnp.int32)
    same_target = (target_rank[:, None] == target_rank[None, :]) & (local[None, :] < local[:, None])
    position = target_rank * pair + jnp.sum(same_target.astype(jnp.int32), axis=1)
    hits = local[:, None] == position[None, :]
    source = jnp.sum(jnp.where(hits, local[None, :], 0), axis=1)
    sent_length = jnp.sum(jnp.where(hits, seq_len[None, :], 0), axis=1)
    tok = jnp.take(hidden, source, axis=0).reshape(ranks, 2, pair // 2 * length, width)
    lens = jnp.broadcast_to(
        sent_length.astype(jnp.float32).reshape(ranks, 1, pair, 1), (ranks, 8, pair, length)
    ).reshape(ranks, 8, pair * length)

    head = query_gain.shape[0]
    rows, groups, span = joined_projection_weight.shape
    group_query = span - 2 * head
    query_cols = group_query // lax.axis_size("sub")
    core = lax.axis_index("sub")
    gain = lax.dynamic_slice_in_dim(in_gain, lax.axis_index("dp") * rows, rows, 0)
    own_query = lax.dynamic_slice_in_dim(joined_projection_weight, core * query_cols, query_cols, 2)
    own_kv = lax.dynamic_slice_in_dim(
        joined_projection_weight, group_query + core * head, head, 2
    )
    columns = [own_kv[:, i] for i in range(groups)] + [own_query[:, i] for i in range(groups)]
    flat = jnp.concatenate(columns, axis=1).astype(jnp.float32) * gain[:, None]
    w = flat.astype(jnp.bfloat16).reshape(rows, -1, CHUNK).transpose(1, 0, 2)

    q, kv, lengths = exchange(tok, lens, w)
    share = length // lax.axis_size("sub")
    key_share, value_share, context = attend(q, kv, lengths, query_gain, k_gain, length, share)
    return (key_share, value_share, context.reshape(slots, length, groups, query_cols))


def solution(mesh):
    sizes = mesh.shape
    paired = (
        sizes["dp"] == 4 and sizes["tensor"] == 2 and sizes["sub"] == 2 and sizes["groups"] == 2
    )
    placed = (
        P(("groups", "dp"), None, ("tensor", "sub")),
        P(("groups", "dp")),
        P(("groups", "dp")),
        P(),
        P("dp", "tensor", None),
        P(),
        P(),
    )
    return jax.shard_map(
        paired_body if paired else body,
        mesh=mesh,
        in_specs=placed,
        out_specs=(
            P(("groups", "dp"), "sub", "tensor"),
            P(("groups", "dp"), "sub", "tensor"),
            P(("groups", "dp"), None, "tensor", "sub"),
        ),
        check_vma=False,
    )
```

```python
import functools

import jax
import jax.numpy as jnp
from jax import lax
from jax.experimental import pallas as pl
from jax.experimental.pallas import tpu as pltpu
from jax.sharding import PartitionSpec as P

EPS = 1e-06
THETA = 1000000.0


def per_head_norm(value_rows, gain):
    square_mean = jnp.mean(value_rows * value_rows, axis=-1, keepdims=True)
    return value_rows * lax.rsqrt(square_mean + EPS) * gain


def rotary_embed(value_rows, token_positions):
    half_width = value_rows.shape[-1] // 2
    frequency = THETA ** (-(2.0 * jnp.arange(half_width, dtype=jnp.float32)) / value_rows.shape[-1])
    angle = token_positions.astype(jnp.float32)[:, None] * frequency[None, :]
    cosine = jnp.cos(angle)[None, :, None, :]
    sine = jnp.sin(angle)[None, :, None, :]
    first = value_rows[..., :half_width]
    second = value_rows[..., half_width:]
    return jnp.concatenate(
        [first * cosine - second * sine, second * cosine + first * sine], axis=-1
    )


def body(hidden, seq_len, target_rank, in_gain, joined_projection_weight, query_gain, k_gain):
    slots, length, width = hidden.shape
    ranks = lax.axis_size("dp")
    pair = -(-slots // ranks)
    lanes = ranks * pair
    local = jnp.arange(slots, dtype=jnp.int32)
    same_target = (target_rank[:, None] == target_rank[None, :]) & (local[None, :] < local[:, None])
    earlier = jnp.sum(same_target.astype(jnp.int32), axis=1)
    position = target_rank * pair + earlier
    lane_ids = jnp.arange(lanes, dtype=jnp.int32)
    hits = lane_ids[:, None] == position[None, :]
    filled = jnp.any(hits, axis=1)
    source = jnp.sum(jnp.where(hits, local[None, :], 0), axis=1)
    outgoing = jnp.where(
        filled[:, None, None], jnp.take(hidden, source, axis=0), jnp.zeros((), hidden.dtype)
    )
    sent_length = jnp.where(filled, jnp.take(seq_len, source), 0)
    arrived, arrived_length = (
        lax.all_to_all(
            outgoing.reshape(ranks, pair, length, width),
            "dp",
            split_axis=0,
            concat_axis=0,
            tiled=True,
        ),
        lax.all_to_all(
            sent_length.reshape(ranks, pair), "dp", split_axis=0, concat_axis=0, tiled=True
        ),
    )
    arrived = arrived.reshape(lanes, length, width)
    arrived_length = arrived_length.reshape(lanes)
    present = arrived_length > 0
    arrived_slot = jnp.cumsum(present.astype(jnp.int32)) - 1
    matches = (arrived_slot[None, :] == local[:, None]) & present[None, :]
    chosen = jnp.sum(jnp.where(matches, lane_ids[None, :], 0), axis=1)
    lengths = jnp.sum(jnp.where(matches, arrived_length[None, :], 0), axis=1)
    moved = arrived if lanes == slots else jnp.take(arrived, chosen, axis=0)
    whole = lax.all_gather(moved, ("tensor", "sub"), axis=2, tiled=True)
    tokens = whole.reshape(slots * length, whole.shape[2]).astype(jnp.float32)
    square_mean = jnp.mean(tokens * tokens, axis=-1, keepdims=True)
    normed_query = (tokens * lax.rsqrt(square_mean + EPS) * in_gain).astype(jnp.bfloat16)
    groups = joined_projection_weight.shape[1]
    head_dim = query_gain.shape[0]
    group_query = joined_projection_weight.shape[2] - 2 * head_dim
    half_heads = group_query // head_dim // lax.axis_size("sub")
    query_cols = half_heads * head_dim
    core = lax.axis_index("sub")
    own_query = lax.dynamic_slice_in_dim(joined_projection_weight, core * query_cols, query_cols, 2)
    extra = joined_projection_weight[:, :, group_query:]
    columns = jnp.concatenate([own_query, extra], axis=2)
    span = columns.shape[2]
    flat_columns = columns.reshape(columns.shape[0], groups * span)
    copies = lax.axis_size("groups")
    rows = flat_columns.shape[0] // copies
    own_rows = lax.dynamic_slice_in_dim(flat_columns, lax.axis_index("groups") * rows, rows, 0)
    mixed_projection = jnp.dot(
        normed_query,
        lax.all_gather(own_rows, ("dp", "groups"), axis=0, tiled=True),
        preferred_element_type=jnp.float32,
    )
    mixed_projection = mixed_projection.reshape(slots, length, groups, span)
    token_positions = jnp.arange(length, dtype=jnp.int32)
    live = token_positions[None, :] < lengths[:, None]
    query_rows = mixed_projection[..., :query_cols].reshape(
        slots, length, groups * half_heads, head_dim
    )
    query_rows = rotary_embed(per_head_norm(query_rows, query_gain), token_positions).astype(
        jnp.bfloat16
    )
    key_rows = rotary_embed(
        per_head_norm(mixed_projection[..., query_cols : query_cols + head_dim], k_gain),
        token_positions,
    )
    key_rows = jnp.where(live[:, :, None, None], key_rows, 0.0).astype(jnp.bfloat16)
    value_rows = jnp.where(
        live[:, :, None, None], mixed_projection[..., query_cols + head_dim :], 0.0
    ).astype(jnp.bfloat16)
    grouped_heads = query_rows.reshape(slots, length, groups, half_heads, head_dim)
    scores = jnp.einsum(
        "nqghd,nkgd->nghqk", grouped_heads, key_rows, preferred_element_type=jnp.float32
    ) * head_dim ** (-0.5)
    causal = token_positions[None, :] <= token_positions[:, None]
    allowed = causal[None, None, None, :, :] & live[:, None, None, None, :]
    weights = jnp.where(allowed, jnp.exp(scores), 0.0)
    probs = (weights / jnp.sum(weights, axis=-1, keepdims=True)).astype(jnp.bfloat16)
    context = jnp.einsum("nghqk,nkgd->nqghd", probs, value_rows, preferred_element_type=jnp.float32)
    context = jnp.where(live[:, :, None, None, None], context, 0.0)
    context = context.reshape(slots, length, groups, half_heads * head_dim).astype(jnp.bfloat16)
    share = length // lax.axis_size("sub")
    key_share = lax.dynamic_slice_in_dim(key_rows, core * share, share, 1).reshape(
        slots, share, groups * head_dim
    )
    value_share = lax.dynamic_slice_in_dim(value_rows, core * share, share, 1).reshape(
        slots, share, groups * head_dim
    )
    return (key_share, value_share, context)


CHUNK = 256


def exchange_kernel(
    tok, lens, w, q_out, kv_out, len_out,
    a, wm, psend, prec, own, ssend, srecv, scales, kvown, kvrecv, lrecv,
    s1s, s1r, s2s, s2r, s3s, s3r, s4s, s4r,
    ws, wr, wfs, wfr, ps, pr, ss, sr, ls, lr, kvs, kvr,
):
    g = lax.axis_index("groups")
    z = lax.axis_index("dp")
    x = lax.axis_index("tensor")
    s = lax.axis_index("sub")
    here = z % 2
    pair = z // 2
    half = w.shape[1] // 2
    n_chunks = w.shape[0]
    x_mate = (g, z, 1 - x, s)
    sibling = (g, z, x, 1 - s)
    z_mate = (g, pair * 2 + (1 - here), x, s)
    y_mate = (1 - g, z, x, s)
    far = (g, (1 - pair) * 2 + here, x, s)

    barrier = pltpu.get_barrier_semaphore()
    for dz in range(1, 4):
        for dx in range(2):
            pl.semaphore_signal(
                barrier, inc=1, device_id=(g, (z + dz) % 4, (x + dx) % 2, s),
                device_id_type=pl.DeviceIdType.MESH,
            )
    for other in (x_mate, sibling, y_mate):
        pl.semaphore_signal(barrier, inc=1, device_id=other, device_id_type=pl.DeviceIdType.MESH)
    pl.semaphore_wait(barrier, 9)

    def remote(src, dst, send, recv, device):
        return pltpu.make_async_remote_copy(
            src_ref=src, dst_ref=dst, send_sem=send, recv_sem=recv,
            device_id=device, device_id_type=pl.DeviceIdType.MESH,
        )

    def first(o, b, h):
        target = 2 * ((x + 1 + o) % 2) + b
        src = tok.at[target, h]
        dst = a.at[o, s, z, h]
        zt = 2 * x + b
        stays = (zt == z) & (x == h)
        return (
            stays,
            remote(src, dst, s1s.at[o, b, h], s1r.at[o, z], (g, zt, h, s)),
            pltpu.make_async_copy(src, dst, s1r.at[o, z]),
        )

    def start_first(o):
        for b in range(2):
            for h in range(2):
                stays, away, local = first(o, b, h)
                pl.when(jnp.logical_not(stays))(away.start)
                pl.when(stays)(local.start)

    def arrived(o, zs):
        dst = a.at[o, s, zs, x]
        local = (pair == x) & (z == zs)
        pl.when(jnp.logical_not(local))(
            remote(dst, dst, s1s.at[o, 0, 0], s1r.at[o, zs], x_mate).wait_recv
        )
        pl.when(local)(pltpu.make_async_copy(tok.at[0, 0], dst, s1r.at[o, zs]).wait)

    def to_x(o, zs):
        piece = a.at[o, s, zs, x]
        return remote(piece, piece, s2s.at[o, zs], s2r.at[o, zs], x_mate)

    def from_x(o, zs):
        piece = a.at[o, s, zs, 1 - x]
        return remote(piece, piece, s2s.at[o, zs], s2r.at[o, zs], x_mate)

    def to_sub(o, zs):
        piece = a.at[o, s, zs, x]
        return remote(piece, piece, s3s.at[o, zs], s3r.at[o, zs], sibling)

    def from_sub(o, zs):
        piece = a.at[o, 1 - s, zs, x]
        return remote(piece, piece, s3s.at[o, zs], s3r.at[o, zs], sibling)

    def to_sub_late(o, zs):
        piece = a.at[o, s, zs, 1 - x]
        return remote(piece, piece, s4s.at[o, zs], s4r.at[o, zs], sibling)

    def from_sub_late(o, zs):
        piece = a.at[o, 1 - s, zs, 1 - x]
        return remote(piece, piece, s4s.at[o, zs], s4r.at[o, zs], sibling)

    def forward(o, after):
        for zs in range(4):
            arrived(o, zs)
            to_x(o, zs).start()
            to_sub(o, zs).start()
        after()
        for zs in range(4):
            from_x(o, zs).wait_recv()
            to_sub_late(o, zs).start()
        for zs in range(4):
            from_sub(o, zs).wait_recv()
            from_sub_late(o, zs).wait_recv()

    def w_copy(c):
        rows = pl.ds(pl.multiple_of(g * half, half), half)
        return remote(w.at[c, rows], wm.at[c, rows], ws.at[c], wr.at[c], z_mate)

    def w_forward(c):
        rows = pl.ds(pl.multiple_of(g * half, half), half)
        return remote(wm.at[c, rows], wm.at[c, rows], wfs.at[c], wfr.at[c], y_mate)

    def w_forwarded(c):
        rows = pl.ds(pl.multiple_of((1 - g) * half, half), half)
        return remote(wm.at[c, rows], wm.at[c, rows], wfs.at[c], wfr.at[c], y_mate)

    def p_copy(c):
        return remote(psend.at[c], prec.at[c], ps.at[c], pr.at[c], far)

    def s_copy():
        return remote(ssend, srecv, ss.at[0], sr.at[0], far)

    def kv_copy():
        return remote(kvown, kvrecv, kvs.at[0], kvr.at[0], sibling)

    def len_copy(step):
        zt = (z + step) % 4
        return remote(lens.at[zt], lrecv.at[z], ls.at[step], lr.at[step], (g, zt, x, s))

    def product(o, c):
        def tokens(block):
            t = a[o, block]
            return t.reshape(t.shape[0] * t.shape[1] * t.shape[2], t.shape[3])

        return jnp.dot(
            tokens(here), w[c], preferred_element_type=jnp.float32
        ) + jnp.dot(tokens(1 - here), wm[c], preferred_element_type=jnp.float32)

    def squares(o, zs):
        total = None
        for block in range(2):
            t = a[o, block, zs].reshape(128, a.shape[5]).astype(jnp.float32)
            part = jnp.sum(t * t, axis=1, keepdims=True)
            total = part if total is None else total + part
        return total

    start_first(0)
    for step in range(1, 4):
        len_copy(step).start()
    for c in range(2):
        w_copy(c).start()

    forward(0, lambda: [w_copy(c).start() for c in range(2, n_chunks)])

    w_copy(0).wait_recv()
    w_forward(0).start()

    def send_partial(c):
        w_forwarded(c).wait_recv()
        psend[c] = product(0, c).astype(psend.dtype)
        p_copy(c).start()

    @pl.loop(1, n_chunks)
    def _(c):
        w_copy(c).wait_recv()
        w_forward(c).start()
        pl.when(c == n_chunks - 1)(lambda: start_first(1))
        send_partial(c - 1)

    send_partial(n_chunks - 1)

    @pl.loop(0, 4)
    def _(zs):
        ssend[zs] = jnp.broadcast_to(squares(0, zs), (128, 128)).T[:8]

    s_copy().start()

    forward(1, lambda: None)

    @pl.loop(0, n_chunks)
    def _(c):
        own[c] = product(1, c)

    s_copy().wait_recv()

    @pl.loop(0, 4)
    def _(zs):
        rows = pl.ds(pl.multiple_of(zs * 128, 128), 128)
        total = squares(1, zs) + jnp.broadcast_to(srecv[zs, 0:1], (128, 128)).T
        scales[rows, :] = lax.rsqrt(total / (4 * a.shape[5]) + EPS)

    scale = jnp.concatenate([scales[...]] * (CHUNK // 128), axis=1)
    p_copy(0).wait_recv()
    kvown[...] = (own[0] + prec[0].astype(jnp.float32)) * scale
    kv_copy().start()
    kv_out[s] = kvown[...]

    @pl.loop(1, n_chunks)
    def _(c):
        p_copy(c).wait_recv()
        wide = jnp.concatenate([scales[...]] * (CHUNK // 128), axis=1)
        q_out[c - 1] = (own[c] + prec[c].astype(jnp.float32)) * wide

    len_out[z] = lens[z]
    for step in range(1, 4):
        source = (z + 4 - step) % 4
        remote(lrecv.at[source], lrecv.at[source], ls.at[step], lr.at[step], x_mate).wait_recv()
        len_out[source] = lrecv[source]

    kv_copy().wait_recv()
    kv_out[1 - s] = kvrecv[...]

    for o in range(2):
        for b in range(2):
            for h in range(2):
                stays, away, _ = first(o, b, h)
                pl.when(jnp.logical_not(stays))(away.wait_send)
        for zs in range(4):
            to_x(o, zs).wait_send()
            to_sub(o, zs).wait_send()
            to_sub_late(o, zs).wait_send()
    for c in range(n_chunks):
        w_copy(c).wait_send()
        w_forward(c).wait_send()
        p_copy(c).wait_send()
    s_copy().wait_send()
    kv_copy().wait_send()
    for step in range(1, 4):
        len_copy(step).wait_send()


def exchange(tok, lens, w):
    chunks, width, columns = w.shape
    tokens = tok.shape[0] * tok.shape[1] * tok.shape[2]
    dma = pltpu.SemaphoreType.DMA
    vmem = pl.BlockSpec(memory_space=pltpu.VMEM)
    f32 = jnp.float32
    bf16 = jnp.bfloat16
    return pl.pallas_call(
        exchange_kernel,
        out_shape=(
            jax.ShapeDtypeStruct((chunks - 1, tokens, columns), f32),
            jax.ShapeDtypeStruct((2, tokens, columns), f32),
            jax.ShapeDtypeStruct(lens.shape, f32),
        ),
        in_specs=[pl.BlockSpec(memory_space=pl.ANY), vmem, vmem],
        out_specs=(vmem, vmem, vmem),
        scratch_shapes=[
            pltpu.VMEM((2, 2, 4, 2, tok.shape[2], width), bf16),
            pltpu.VMEM((chunks, width, columns), bf16),
            pltpu.VMEM((chunks, tokens, columns), bf16),
            pltpu.VMEM((chunks, tokens, columns), bf16),
            pltpu.VMEM((chunks, tokens, columns), f32),
            pltpu.VMEM(lens.shape, f32),
            pltpu.VMEM(lens.shape, f32),
            pltpu.VMEM((tokens, 128), f32),
            pltpu.VMEM((tokens, columns), f32),
            pltpu.VMEM((tokens, columns), f32),
            pltpu.VMEM(lens.shape, f32),
            dma((2, 2, 2)), dma((2, 4)), dma((2, 4)), dma((2, 4)),
            dma((2, 4)), dma((2, 4)), dma((2, 4)), dma((2, 4)),
            dma((chunks,)), dma((chunks,)), dma((chunks,)), dma((chunks,)),
            dma((chunks,)), dma((chunks,)), dma((1,)), dma((1,)),
            dma((4,)), dma((4,)), dma((1,)), dma((1,)),
        ],
        compiler_params=pltpu.CompilerParams(
            collective_id=0, has_side_effects=True, vmem_limit_bytes=48 << 20
        ),
        cost_estimate=pl.CostEstimate(
            flops=8 * tokens * width * chunks * columns, bytes_accessed=1 << 24, transcendentals=0
        ),
        name="exchange",
    )(tok, lens, w)


def attend_kernel(q_ref, kv_ref, len_ref, cos_ref, sin_ref, qg_ref, kg_ref, k_out, v_out, ctx_out):
    head = cos_ref.shape[1]
    rows = cos_ref.shape[0]
    seqs, share, _ = k_out.shape
    length = rows // seqs
    core = lax.axis_index("sub")
    len_key = jnp.broadcast_to(len_ref[0, 0:1, :], (rows, rows))
    len_query = len_key.T
    row_ids = lax.broadcasted_iota(jnp.int32, (rows, rows), 0)
    col_ids = lax.broadcasted_iota(jnp.int32, (rows, rows), 1)
    key_pos = (col_ids % length).astype(jnp.float32)
    query_pos = (row_ids % length).astype(jnp.float32)
    allowed = (
        (row_ids // length == col_ids // length) & (col_ids <= row_ids) & (key_pos < len_key)
    )
    live = query_pos < len_query
    cos = cos_ref[...]
    sin = sin_ref[...]

    def norm_rope(t, gain):
        mean = jnp.mean(t * t, axis=-1, keepdims=True)
        t = t * lax.rsqrt(mean + EPS) * gain
        return t * cos + pltpu.roll(t, head // 2, 1) * sin

    def part(t):
        t = t.reshape(seqs, length, head)
        return jnp.where(core == 0, t[:, :share], t[:, share:])

    kgain = kg_ref[...]
    qgain = qg_ref[...]
    n_groups = kv_ref.shape[2] // head
    heads = q_ref.shape[0] * q_ref.shape[2] // head // n_groups
    per_chunk = q_ref.shape[2] // head
    for group in range(n_groups):
        cols = slice(group * head, (group + 1) * head)
        key = jnp.where(live, norm_rope(kv_ref[0, :, cols], kgain), 0.0)
        value = jnp.where(live, kv_ref[1, :, cols], 0.0)
        k_out[:, :, cols] = part(key).astype(k_out.dtype)
        v_out[:, :, cols] = part(value).astype(v_out.dtype)
        key = key.astype(jnp.bfloat16)
        value = value.astype(jnp.bfloat16)
        for h in range(heads):
            n = group * heads + h
            at = n % per_chunk * head
            query = norm_rope(q_ref[n // per_chunk, :, at : at + head], qgain)
            scores = lax.dot_general(
                query.astype(jnp.bfloat16), key, (((1,), (1,)), ((), ())),
                preferred_element_type=jnp.float32,
            ) * head ** (-0.5)
            weights = jnp.where(allowed, jnp.exp(scores), 0.0)
            probs = weights / jnp.sum(weights, axis=-1, keepdims=True)
            out = jnp.dot(probs.astype(jnp.bfloat16), value, preferred_element_type=jnp.float32)
            ctx_out[:, n * head : (n + 1) * head] = jnp.where(live, out, 0.0).astype(ctx_out.dtype)


def attend(q, kv, lens, query_gain, k_gain, length, share):
    head = query_gain.shape[0]
    chunks, tokens, columns = q.shape
    blocks = lens.shape[0]
    rows = tokens // blocks
    seqs = rows // length
    frequency = THETA ** (-(2.0 * jnp.arange(head // 2, dtype=jnp.float32)) / head)
    positions = jnp.arange(rows, dtype=jnp.int32) % length
    angle = positions.astype(jnp.float32)[:, None] * frequency[None, :]
    cos = jnp.cos(angle)
    sin = jnp.sin(angle)
    whole = lambda *shape: pl.BlockSpec(shape, lambda i: (0,) * len(shape))
    cache = jax.ShapeDtypeStruct((tokens // length, share, columns), jnp.bfloat16)
    return pl.pallas_call(
        attend_kernel,
        grid=(blocks,),
        out_shape=(cache, cache, jax.ShapeDtypeStruct((tokens, chunks * columns), jnp.bfloat16)),
        in_specs=[
            pl.BlockSpec((chunks, rows, columns), lambda i: (0, i, 0)),
            pl.BlockSpec((2, rows, columns), lambda i: (0, i, 0)),
            pl.BlockSpec((1,) + lens.shape[1:], lambda i: (i, 0, 0)),
            whole(rows, head), whole(rows, head), whole(1, head), whole(1, head),
        ],
        out_specs=(
            pl.BlockSpec((seqs, share, columns), lambda i: (i, 0, 0)),
            pl.BlockSpec((seqs, share, columns), lambda i: (i, 0, 0)),
            pl.BlockSpec((rows, chunks * columns), lambda i: (i, 0)),
        ),
        compiler_params=pltpu.CompilerParams(vmem_limit_bytes=32 << 20),
        name="attend",
    )(
        q, kv, lens,
        jnp.concatenate([cos, cos], axis=1), jnp.concatenate([-sin, sin], axis=1),
        query_gain[None, :], k_gain[None, :],
    )


def paired_body(
    hidden, seq_len, target_rank, in_gain, joined_projection_weight, query_gain, k_gain
):
    slots, length, width = hidden.shape
    ranks = lax.axis_size("dp")
    pair = slots // ranks
    local = jnp.arange(slots, dtype=jnp.int32)
    same_target = (target_rank[:, None] == target_rank[None, :]) & (local[None, :] < local[:, None])
    position = target_rank * pair + jnp.sum(same_target.astype(jnp.int32), axis=1)
    hits = local[:, None] == position[None, :]
    source = jnp.sum(jnp.where(hits, local[None, :], 0), axis=1)
    sent_length = jnp.sum(jnp.where(hits, seq_len[None, :], 0), axis=1)
    tok = jnp.take(hidden, source, axis=0, mode="clip").reshape(ranks, 2, pair // 2 * length, width)
    lens = jnp.broadcast_to(
        sent_length.astype(jnp.float32).reshape(ranks, 1, pair, 1), (ranks, 8, pair, length)
    ).reshape(ranks, 8, pair * length)

    head = query_gain.shape[0]
    rows, groups, span = joined_projection_weight.shape
    group_query = span - 2 * head
    query_cols = group_query // lax.axis_size("sub")
    core = lax.axis_index("sub")
    gain = lax.dynamic_slice_in_dim(in_gain, lax.axis_index("dp") * rows, rows, 0)
    own_query = lax.dynamic_slice_in_dim(joined_projection_weight, core * query_cols, query_cols, 2)
    own_kv = lax.dynamic_slice_in_dim(
        joined_projection_weight, group_query + core * head, head, 2
    )
    columns = [jnp.concatenate([own_kv[:, i] for i in range(groups)], axis=1)] + [
        own_query[:, i, at : at + CHUNK] for i in range(groups) for at in range(0, query_cols, CHUNK)
    ]
    w = (jnp.stack(columns).astype(jnp.float32) * gain[None, :, None]).astype(jnp.bfloat16)

    q, kv, lengths = exchange(tok, lens, w)
    share = length // lax.axis_size("sub")
    key_share, value_share, context = attend(q, kv, lengths, query_gain, k_gain, length, share)
    return (key_share, value_share, context.reshape(slots, length, groups, query_cols))


def solution(mesh):
    sizes = mesh.shape
    paired = (
        sizes["dp"] == 4 and sizes["tensor"] == 2 and sizes["sub"] == 2 and sizes["groups"] == 2
    )
    placed = (
        P(("groups", "dp"), None, ("tensor", "sub")),
        P(("groups", "dp")),
        P(("groups", "dp")),
        P(),
        P("dp", "tensor", None),
        P(),
        P(),
    )
    return jax.shard_map(
        paired_body if paired else body,
        mesh=mesh,
        in_specs=placed,
        out_specs=(
            P(("groups", "dp"), "sub", "tensor"),
            P(("groups", "dp"), "sub", "tensor"),
            P(("groups", "dp"), None, "tensor", "sub"),
        ),
        check_vma=False,
    )
```

```python
import functools

import jax
import jax.numpy as jnp
from jax import lax
from jax.experimental import pallas as pl
from jax.experimental.pallas import tpu as pltpu
from jax.sharding import PartitionSpec as P

EPS = 1e-06
THETA = 1000000.0


def per_head_norm(value_rows, gain):
    square_mean = jnp.mean(value_rows * value_rows, axis=-1, keepdims=True)
    return value_rows * lax.rsqrt(square_mean + EPS) * gain


def rotary_embed(value_rows, token_positions):
    half_width = value_rows.shape[-1] // 2
    frequency = THETA ** (-(2.0 * jnp.arange(half_width, dtype=jnp.float32)) / value_rows.shape[-1])
    angle = token_positions.astype(jnp.float32)[:, None] * frequency[None, :]
    cosine = jnp.cos(angle)[None, :, None, :]
    sine = jnp.sin(angle)[None, :, None, :]
    first = value_rows[..., :half_width]
    second = value_rows[..., half_width:]
    return jnp.concatenate(
        [first * cosine - second * sine, second * cosine + first * sine], axis=-1
    )


def body(hidden, seq_len, target_rank, in_gain, joined_projection_weight, query_gain, k_gain):
    slots, length, width = hidden.shape
    ranks = lax.axis_size("dp")
    pair = -(-slots // ranks)
    lanes = ranks * pair
    local = jnp.arange(slots, dtype=jnp.int32)
    same_target = (target_rank[:, None] == target_rank[None, :]) & (local[None, :] < local[:, None])
    earlier = jnp.sum(same_target.astype(jnp.int32), axis=1)
    position = target_rank * pair + earlier
    lane_ids = jnp.arange(lanes, dtype=jnp.int32)
    hits = lane_ids[:, None] == position[None, :]
    filled = jnp.any(hits, axis=1)
    source = jnp.sum(jnp.where(hits, local[None, :], 0), axis=1)
    outgoing = jnp.where(
        filled[:, None, None], jnp.take(hidden, source, axis=0), jnp.zeros((), hidden.dtype)
    )
    sent_length = jnp.where(filled, jnp.take(seq_len, source), 0)
    arrived, arrived_length = (
        lax.all_to_all(
            outgoing.reshape(ranks, pair, length, width),
            "dp",
            split_axis=0,
            concat_axis=0,
            tiled=True,
        ),
        lax.all_to_all(
            sent_length.reshape(ranks, pair), "dp", split_axis=0, concat_axis=0, tiled=True
        ),
    )
    arrived = arrived.reshape(lanes, length, width)
    arrived_length = arrived_length.reshape(lanes)
    present = arrived_length > 0
    arrived_slot = jnp.cumsum(present.astype(jnp.int32)) - 1
    matches = (arrived_slot[None, :] == local[:, None]) & present[None, :]
    chosen = jnp.sum(jnp.where(matches, lane_ids[None, :], 0), axis=1)
    lengths = jnp.sum(jnp.where(matches, arrived_length[None, :], 0), axis=1)
    moved = arrived if lanes == slots else jnp.take(arrived, chosen, axis=0)
    whole = lax.all_gather(moved, ("tensor", "sub"), axis=2, tiled=True)
    tokens = whole.reshape(slots * length, whole.shape[2]).astype(jnp.float32)
    square_mean = jnp.mean(tokens * tokens, axis=-1, keepdims=True)
    normed_query = (tokens * lax.rsqrt(square_mean + EPS) * in_gain).astype(jnp.bfloat16)
    groups = joined_projection_weight.shape[1]
    head_dim = query_gain.shape[0]
    group_query = joined_projection_weight.shape[2] - 2 * head_dim
    half_heads = group_query // head_dim // lax.axis_size("sub")
    query_cols = half_heads * head_dim
    core = lax.axis_index("sub")
    own_query = lax.dynamic_slice_in_dim(joined_projection_weight, core * query_cols, query_cols, 2)
    extra = joined_projection_weight[:, :, group_query:]
    columns = jnp.concatenate([own_query, extra], axis=2)
    span = columns.shape[2]
    flat_columns = columns.reshape(columns.shape[0], groups * span)
    copies = lax.axis_size("groups")
    rows = flat_columns.shape[0] // copies
    own_rows = lax.dynamic_slice_in_dim(flat_columns, lax.axis_index("groups") * rows, rows, 0)
    mixed_projection = jnp.dot(
        normed_query,
        lax.all_gather(own_rows, ("dp", "groups"), axis=0, tiled=True),
        preferred_element_type=jnp.float32,
    )
    mixed_projection = mixed_projection.reshape(slots, length, groups, span)
    token_positions = jnp.arange(length, dtype=jnp.int32)
    live = token_positions[None, :] < lengths[:, None]
    query_rows = mixed_projection[..., :query_cols].reshape(
        slots, length, groups * half_heads, head_dim
    )
    query_rows = rotary_embed(per_head_norm(query_rows, query_gain), token_positions).astype(
        jnp.bfloat16
    )
    key_rows = rotary_embed(
        per_head_norm(mixed_projection[..., query_cols : query_cols + head_dim], k_gain),
        token_positions,
    )
    key_rows = jnp.where(live[:, :, None, None], key_rows, 0.0).astype(jnp.bfloat16)
    value_rows = jnp.where(
        live[:, :, None, None], mixed_projection[..., query_cols + head_dim :], 0.0
    ).astype(jnp.bfloat16)
    grouped_heads = query_rows.reshape(slots, length, groups, half_heads, head_dim)
    scores = jnp.einsum(
        "nqghd,nkgd->nghqk", grouped_heads, key_rows, preferred_element_type=jnp.float32
    ) * head_dim ** (-0.5)
    causal = token_positions[None, :] <= token_positions[:, None]
    allowed = causal[None, None, None, :, :] & live[:, None, None, None, :]
    weights = jnp.where(allowed, jnp.exp(scores), 0.0)
    probs = (weights / jnp.sum(weights, axis=-1, keepdims=True)).astype(jnp.bfloat16)
    context = jnp.einsum("nghqk,nkgd->nqghd", probs, value_rows, preferred_element_type=jnp.float32)
    context = jnp.where(live[:, :, None, None, None], context, 0.0)
    context = context.reshape(slots, length, groups, half_heads * head_dim).astype(jnp.bfloat16)
    share = length // lax.axis_size("sub")
    key_share = lax.dynamic_slice_in_dim(key_rows, core * share, share, 1).reshape(
        slots, share, groups * head_dim
    )
    value_share = lax.dynamic_slice_in_dim(value_rows, core * share, share, 1).reshape(
        slots, share, groups * head_dim
    )
    return (key_share, value_share, context)


CHUNK = 256


def exchange_kernel(
    tok, lens, w, q_out, kv_out, len_out,
    a, wm, psend, prec, own, ssend, srecv, scales, kvown, kvrecv, lrecv,
    s1s, s1r, s2s, s2r, s3s, s3r, s4s, s4r,
    ws, wr, wfs, wfr, ps, pr, ss, sr, ls, lr, kvs, kvr,
):
    g = lax.axis_index("groups")
    z = lax.axis_index("dp")
    x = lax.axis_index("tensor")
    s = lax.axis_index("sub")
    here = z % 2
    pair = z // 2
    half = w.shape[0] // 2
    n_chunks = wm.shape[0]
    x_mate = (g, z, 1 - x, s)
    sibling = (g, z, x, 1 - s)
    z_mate = (g, pair * 2 + (1 - here), x, s)
    y_mate = (1 - g, z, x, s)
    far = (g, (1 - pair) * 2 + here, x, s)

    barrier = pltpu.get_barrier_semaphore()
    for dz in range(1, 4):
        for dx in range(2):
            pl.semaphore_signal(
                barrier, inc=1, device_id=(g, (z + dz) % 4, (x + dx) % 2, s),
                device_id_type=pl.DeviceIdType.MESH,
            )
    for other in (x_mate, sibling, y_mate):
        pl.semaphore_signal(barrier, inc=1, device_id=other, device_id_type=pl.DeviceIdType.MESH)
    pl.semaphore_wait(barrier, 9)

    def remote(src, dst, send, recv, device):
        return pltpu.make_async_remote_copy(
            src_ref=src, dst_ref=dst, send_sem=send, recv_sem=recv,
            device_id=device, device_id_type=pl.DeviceIdType.MESH,
        )

    def first(o, b, h):
        target = 2 * ((x + 1 + o) % 2) + b
        src = tok.at[target, h]
        dst = a.at[o, s, z, h]
        zt = 2 * x + b
        stays = (zt == z) & (x == h)
        return (
            stays,
            remote(src, dst, s1s.at[o, b, h], s1r.at[o, z], (g, zt, h, s)),
            pltpu.make_async_copy(src, dst, s1r.at[o, z]),
        )

    def start_first(o):
        for b in range(2):
            for h in range(2):
                stays, away, local = first(o, b, h)
                pl.when(jnp.logical_not(stays))(away.start)
                pl.when(stays)(local.start)

    def arrived(o, zs):
        dst = a.at[o, s, zs, x]
        local = (pair == x) & (z == zs)
        pl.when(jnp.logical_not(local))(
            remote(dst, dst, s1s.at[o, 0, 0], s1r.at[o, zs], x_mate).wait_recv
        )
        pl.when(local)(pltpu.make_async_copy(tok.at[0, 0], dst, s1r.at[o, zs]).wait)

    def to_x(o, zs):
        piece = a.at[o, s, zs, x]
        return remote(piece, piece, s2s.at[o, zs], s2r.at[o, zs], x_mate)

    def from_x(o, zs):
        piece = a.at[o, s, zs, 1 - x]
        return remote(piece, piece, s2s.at[o, zs], s2r.at[o, zs], x_mate)

    def to_sub(o, zs):
        piece = a.at[o, s, zs, x]
        return remote(piece, piece, s3s.at[o, zs], s3r.at[o, zs], sibling)

    def from_sub(o, zs):
        piece = a.at[o, 1 - s, zs, x]
        return remote(piece, piece, s3s.at[o, zs], s3r.at[o, zs], sibling)

    def to_sub_late(o, zs):
        piece = a.at[o, s, zs, 1 - x]
        return remote(piece, piece, s4s.at[o, zs], s4r.at[o, zs], sibling)

    def from_sub_late(o, zs):
        piece = a.at[o, 1 - s, zs, 1 - x]
        return remote(piece, piece, s4s.at[o, zs], s4r.at[o, zs], sibling)

    def forward_first(o):
        for zs in range(4):
            arrived(o, zs)
            to_x(o, zs).start()
            to_sub(o, zs).start()

    def forward_second(o):
        for zs in range(4):
            from_x(o, zs).wait_recv()
            to_sub_late(o, zs).start()

    def forward_last(o):
        for zs in range(4):
            from_sub(o, zs).wait_recv()
            from_sub_late(o, zs).wait_recv()

    def w_copy(c):
        rows = pl.ds(pl.multiple_of(g * half, half), half)
        cols = pl.ds(pl.multiple_of(c * CHUNK, CHUNK), CHUNK)
        return remote(w.at[rows, cols], wm.at[c, rows], ws.at[c], wr.at[c], z_mate)

    def w_forward(c):
        rows = pl.ds(pl.multiple_of(g * half, half), half)
        return remote(wm.at[c, rows], wm.at[c, rows], wfs.at[c], wfr.at[c], y_mate)

    def w_forwarded(c):
        rows = pl.ds(pl.multiple_of((1 - g) * half, half), half)
        return remote(wm.at[c, rows], wm.at[c, rows], wfs.at[c], wfr.at[c], y_mate)

    def p_copy(c):
        return remote(psend.at[c], prec.at[c], ps.at[c], pr.at[c], far)

    def s_copy():
        return remote(ssend, srecv, ss.at[0], sr.at[0], far)

    def kv_copy():
        return remote(kvown, kvrecv, kvs.at[0], kvr.at[0], sibling)

    def len_copy(step):
        zt = (z + step) % 4
        return remote(lens.at[zt], lrecv.at[z], ls.at[step], lr.at[step], (g, zt, x, s))

    def product(o, c):
        def tokens(block):
            t = a[o, block]
            return t.reshape(t.shape[0] * t.shape[1] * t.shape[2], t.shape[3])

        cols = pl.ds(pl.multiple_of(c * CHUNK, CHUNK), CHUNK)
        return jnp.dot(
            tokens(here), w[:, cols], preferred_element_type=jnp.float32
        ) + jnp.dot(tokens(1 - here), wm[c], preferred_element_type=jnp.float32)

    def squares(o, zs):
        total = None
        for block in range(2):
            t = a[o, block, zs].reshape(128, a.shape[5]).astype(jnp.float32)
            part = jnp.sum(t * t, axis=1, keepdims=True)
            total = part if total is None else total + part
        return total

    start_first(0)
    for step in range(1, 4):
        len_copy(step).start()
    for c in range(n_chunks):
        w_copy(c).start()

    forward_first(0)
    start_first(1)
    for c in range(n_chunks):
        w_copy(c).wait_recv()
        w_forward(c).start()
    forward_second(0)
    forward_last(0)

    @pl.loop(0, n_chunks)
    def _(c):
        w_forwarded(c).wait_recv()
        psend[c] = product(0, c).astype(psend.dtype)
        p_copy(c).start()
        pl.when(c == 1)(lambda: forward_first(1))
        pl.when(c == 2)(lambda: forward_second(1))

    @pl.loop(0, 4)
    def _(zs):
        ssend[zs] = jnp.broadcast_to(squares(0, zs), (128, 128)).T[:8]

    s_copy().start()

    forward_last(1)

    @pl.loop(0, n_chunks)
    def _(c):
        own[c] = product(1, c)

    s_copy().wait_recv()

    @pl.loop(0, 4)
    def _(zs):
        rows = pl.ds(pl.multiple_of(zs * 128, 128), 128)
        total = squares(1, zs) + jnp.broadcast_to(srecv[zs, 0:1], (128, 128)).T
        scales[rows, :] = lax.rsqrt(total / (4 * a.shape[5]) + EPS)

    scale = jnp.concatenate([scales[...]] * (CHUNK // 128), axis=1)
    p_copy(0).wait_recv()
    kvown[...] = (own[0] + prec[0].astype(jnp.float32)) * scale
    kv_copy().start()
    kv_out[s] = kvown[...]

    @pl.loop(1, n_chunks)
    def _(c):
        p_copy(c).wait_recv()
        wide = jnp.concatenate([scales[...]] * (CHUNK // 128), axis=1)
        q_out[c - 1] = (own[c] + prec[c].astype(jnp.float32)) * wide

    len_out[z] = lens[z]
    for step in range(1, 4):
        source = (z + 4 - step) % 4
        remote(lrecv.at[source], lrecv.at[source], ls.at[step], lr.at[step], x_mate).wait_recv()
        len_out[source] = lrecv[source]

    kv_copy().wait_recv()
    kv_out[1 - s] = kvrecv[...]

    for o in range(2):
        for b in range(2):
            for h in range(2):
                stays, away, _ = first(o, b, h)
                pl.when(jnp.logical_not(stays))(away.wait_send)
        for zs in range(4):
            to_x(o, zs).wait_send()
            to_sub(o, zs).wait_send()
            to_sub_late(o, zs).wait_send()
    for c in range(n_chunks):
        w_copy(c).wait_send()
        w_forward(c).wait_send()
        p_copy(c).wait_send()
    s_copy().wait_send()
    kv_copy().wait_send()
    for step in range(1, 4):
        len_copy(step).wait_send()


def exchange(tok, lens, w):
    width = w.shape[0]
    columns = CHUNK
    chunks = w.shape[1] // columns
    tokens = tok.shape[0] * tok.shape[1] * tok.shape[2]
    dma = pltpu.SemaphoreType.DMA
    vmem = pl.BlockSpec(memory_space=pltpu.VMEM)
    f32 = jnp.float32
    bf16 = jnp.bfloat16
    return pl.pallas_call(
        exchange_kernel,
        out_shape=(
            jax.ShapeDtypeStruct((chunks - 1, tokens, columns), f32),
            jax.ShapeDtypeStruct((2, tokens, columns), f32),
            jax.ShapeDtypeStruct(lens.shape, f32),
        ),
        in_specs=[pl.BlockSpec(memory_space=pl.ANY), vmem, vmem],
        out_specs=(vmem, vmem, vmem),
        scratch_shapes=[
            pltpu.VMEM((2, 2, 4, 2, tok.shape[2], width), bf16),
            pltpu.VMEM((chunks, width, columns), bf16),
            pltpu.VMEM((chunks, tokens, columns), bf16),
            pltpu.VMEM((chunks, tokens, columns), bf16),
            pltpu.VMEM((chunks, tokens, columns), f32),
            pltpu.VMEM(lens.shape, f32),
            pltpu.VMEM(lens.shape, f32),
            pltpu.VMEM((tokens, 128), f32),
            pltpu.VMEM((tokens, columns), f32),
            pltpu.VMEM((tokens, columns), f32),
            pltpu.VMEM(lens.shape, f32),
            dma((2, 2, 2)), dma((2, 4)), dma((2, 4)), dma((2, 4)),
            dma((2, 4)), dma((2, 4)), dma((2, 4)), dma((2, 4)),
            dma((chunks,)), dma((chunks,)), dma((chunks,)), dma((chunks,)),
            dma((chunks,)), dma((chunks,)), dma((1,)), dma((1,)),
            dma((4,)), dma((4,)), dma((1,)), dma((1,)),
        ],
        compiler_params=pltpu.CompilerParams(
            collective_id=0, has_side_effects=True, vmem_limit_bytes=48 << 20
        ),
        cost_estimate=pl.CostEstimate(
            flops=8 * tokens * width * chunks * columns, bytes_accessed=1 << 24, transcendentals=0
        ),
        name="exchange",
    )(tok, lens, w)


def attend_kernel(q_ref, kv_ref, len_ref, cos_ref, sin_ref, qg_ref, kg_ref, k_out, v_out, ctx_out):
    head = cos_ref.shape[1]
    rows = cos_ref.shape[0]
    seqs, share, _ = k_out.shape
    length = rows // seqs
    core = lax.axis_index("sub")
    len_key = jnp.broadcast_to(len_ref[0, 0:1, :], (rows, rows))
    len_query = len_key.T
    row_ids = lax.broadcasted_iota(jnp.int32, (rows, rows), 0)
    col_ids = lax.broadcasted_iota(jnp.int32, (rows, rows), 1)
    key_pos = (col_ids % length).astype(jnp.float32)
    query_pos = (row_ids % length).astype(jnp.float32)
    allowed = (
        (row_ids // length == col_ids // length) & (col_ids <= row_ids) & (key_pos < len_key)
    )
    live = query_pos < len_query
    cos = cos_ref[...]
    sin = sin_ref[...]

    def norm_rope(t, gain):
        mean = jnp.mean(t * t, axis=-1, keepdims=True)
        t = t * lax.rsqrt(mean + EPS) * gain
        return t * cos + pltpu.roll(t, head // 2, 1) * sin

    def part(t):
        t = t.reshape(seqs, length, head)
        return jnp.where(core == 0, t[:, :share], t[:, share:])

    kgain = kg_ref[...]
    qgain = qg_ref[...]
    n_groups = kv_ref.shape[2] // head
    heads = q_ref.shape[0] * q_ref.shape[2] // head // n_groups
    per_chunk = q_ref.shape[2] // head
    for group in range(n_groups):
        cols = slice(group * head, (group + 1) * head)
        key = jnp.where(live, norm_rope(kv_ref[0, :, cols], kgain), 0.0)
        value = jnp.where(live, kv_ref[1, :, cols], 0.0)
        k_out[:, :, cols] = part(key).astype(k_out.dtype)
        v_out[:, :, cols] = part(value).astype(v_out.dtype)
        key = key.astype(jnp.bfloat16)
        value = value.astype(jnp.bfloat16)
        for h in range(heads):
            n = group * heads + h
            at = n % per_chunk * head
            query = norm_rope(q_ref[n // per_chunk, :, at : at + head], qgain)
            scores = lax.dot_general(
                query.astype(jnp.bfloat16), key, (((1,), (1,)), ((), ())),
                preferred_element_type=jnp.float32,
            ) * head ** (-0.5)
            weights = jnp.where(allowed, jnp.exp(scores), 0.0)
            probs = weights / jnp.sum(weights, axis=-1, keepdims=True)
            out = jnp.dot(probs.astype(jnp.bfloat16), value, preferred_element_type=jnp.float32)
            ctx_out[:, n * head : (n + 1) * head] = jnp.where(live, out, 0.0).astype(ctx_out.dtype)


def attend(q, kv, lens, query_gain, k_gain, length, share):
    head = query_gain.shape[0]
    chunks, tokens, columns = q.shape
    blocks = lens.shape[0]
    rows = tokens // blocks
    seqs = rows // length
    frequency = THETA ** (-(2.0 * jnp.arange(head // 2, dtype=jnp.float32)) / head)
    positions = jnp.arange(rows, dtype=jnp.int32) % length
    angle = positions.astype(jnp.float32)[:, None] * frequency[None, :]
    cos = jnp.cos(angle)
    sin = jnp.sin(angle)
    whole = lambda *shape: pl.BlockSpec(shape, lambda i: (0,) * len(shape))
    cache = jax.ShapeDtypeStruct((tokens // length, share, columns), jnp.bfloat16)
    return pl.pallas_call(
        attend_kernel,
        grid=(blocks,),
        out_shape=(cache, cache, jax.ShapeDtypeStruct((tokens, chunks * columns), jnp.bfloat16)),
        in_specs=[
            pl.BlockSpec((chunks, rows, columns), lambda i: (0, i, 0)),
            pl.BlockSpec((2, rows, columns), lambda i: (0, i, 0)),
            pl.BlockSpec((1,) + lens.shape[1:], lambda i: (i, 0, 0)),
            whole(rows, head), whole(rows, head), whole(1, head), whole(1, head),
        ],
        out_specs=(
            pl.BlockSpec((seqs, share, columns), lambda i: (i, 0, 0)),
            pl.BlockSpec((seqs, share, columns), lambda i: (i, 0, 0)),
            pl.BlockSpec((rows, chunks * columns), lambda i: (i, 0)),
        ),
        compiler_params=pltpu.CompilerParams(vmem_limit_bytes=32 << 20),
        name="attend",
    )(
        q, kv, lens,
        jnp.concatenate([cos, cos], axis=1), jnp.concatenate([-sin, sin], axis=1),
        query_gain[None, :], k_gain[None, :],
    )


def paired_body(
    hidden, seq_len, target_rank, in_gain, joined_projection_weight, query_gain, k_gain
):
    slots, length, width = hidden.shape
    ranks = lax.axis_size("dp")
    pair = slots // ranks
    local = jnp.arange(slots, dtype=jnp.int32)
    same_target = (target_rank[:, None] == target_rank[None, :]) & (local[None, :] < local[:, None])
    position = target_rank * pair + jnp.sum(same_target.astype(jnp.int32), axis=1)
    hits = local[:, None] == position[None, :]
    source = jnp.sum(jnp.where(hits, local[None, :], 0), axis=1)
    sent_length = jnp.sum(jnp.where(hits, seq_len[None, :], 0), axis=1)
    tok = jnp.take(hidden, source, axis=0, mode="clip").reshape(ranks, 2, pair // 2 * length, width)
    lens = jnp.broadcast_to(
        sent_length.astype(jnp.float32).reshape(ranks, 1, pair, 1), (ranks, 8, pair, length)
    ).reshape(ranks, 8, pair * length)

    head = query_gain.shape[0]
    rows, groups, span = joined_projection_weight.shape
    group_query = span - 2 * head
    query_cols = group_query // lax.axis_size("sub")
    core = lax.axis_index("sub")
    gain = lax.dynamic_slice_in_dim(in_gain, lax.axis_index("dp") * rows, rows, 0)
    own_query = lax.dynamic_slice_in_dim(joined_projection_weight, core * query_cols, query_cols, 2)
    own_kv = lax.dynamic_slice_in_dim(
        joined_projection_weight, group_query + core * head, head, 2
    )
    columns = [own_kv[:, i] for i in range(groups)] + [own_query[:, i] for i in range(groups)]
    flat = jnp.concatenate(columns, axis=1).astype(jnp.float32) * gain[:, None]
    w = flat.astype(jnp.bfloat16)

    q, kv, lengths = exchange(tok, lens, w)
    share = length // lax.axis_size("sub")
    key_share, value_share, context = attend(q, kv, lengths, query_gain, k_gain, length, share)
    return (key_share, value_share, context.reshape(slots, length, groups, query_cols))


def solution(mesh):
    sizes = mesh.shape
    paired = (
        sizes["dp"] == 4 and sizes["tensor"] == 2 and sizes["sub"] == 2 and sizes["groups"] == 2
    )
    placed = (
        P(("groups", "dp"), None, ("tensor", "sub")),
        P(("groups", "dp")),
        P(("groups", "dp")),
        P(),
        P("dp", "tensor", None),
        P(),
        P(),
    )
    return jax.shard_map(
        paired_body if paired else body,
        mesh=mesh,
        in_specs=placed,
        out_specs=(
            P(("groups", "dp"), "sub", "tensor"),
            P(("groups", "dp"), "sub", "tensor"),
            P(("groups", "dp"), None, "tensor", "sub"),
        ),
        check_vma=False,
    )
```

```python
import functools

import jax
import jax.numpy as jnp
from jax import lax
from jax.experimental import pallas as pl
from jax.experimental.pallas import tpu as pltpu
from jax.sharding import PartitionSpec as P

EPS = 1e-06
THETA = 1000000.0


def per_head_norm(value_rows, gain):
    square_mean = jnp.mean(value_rows * value_rows, axis=-1, keepdims=True)
    return value_rows * lax.rsqrt(square_mean + EPS) * gain


def rotary_embed(value_rows, token_positions):
    half_width = value_rows.shape[-1] // 2
    frequency = THETA ** (-(2.0 * jnp.arange(half_width, dtype=jnp.float32)) / value_rows.shape[-1])
    angle = token_positions.astype(jnp.float32)[:, None] * frequency[None, :]
    cosine = jnp.cos(angle)[None, :, None, :]
    sine = jnp.sin(angle)[None, :, None, :]
    first = value_rows[..., :half_width]
    second = value_rows[..., half_width:]
    return jnp.concatenate(
        [first * cosine - second * sine, second * cosine + first * sine], axis=-1
    )


def body(hidden, seq_len, target_rank, in_gain, joined_projection_weight, query_gain, k_gain):
    slots, length, width = hidden.shape
    ranks = lax.axis_size("dp")
    pair = -(-slots // ranks)
    lanes = ranks * pair
    local = jnp.arange(slots, dtype=jnp.int32)
    same_target = (target_rank[:, None] == target_rank[None, :]) & (local[None, :] < local[:, None])
    earlier = jnp.sum(same_target.astype(jnp.int32), axis=1)
    position = target_rank * pair + earlier
    lane_ids = jnp.arange(lanes, dtype=jnp.int32)
    hits = lane_ids[:, None] == position[None, :]
    filled = jnp.any(hits, axis=1)
    source = jnp.sum(jnp.where(hits, local[None, :], 0), axis=1)
    outgoing = jnp.where(
        filled[:, None, None], jnp.take(hidden, source, axis=0), jnp.zeros((), hidden.dtype)
    )
    sent_length = jnp.where(filled, jnp.take(seq_len, source), 0)
    arrived, arrived_length = (
        lax.all_to_all(
            outgoing.reshape(ranks, pair, length, width),
            "dp",
            split_axis=0,
            concat_axis=0,
            tiled=True,
        ),
        lax.all_to_all(
            sent_length.reshape(ranks, pair), "dp", split_axis=0, concat_axis=0, tiled=True
        ),
    )
    arrived = arrived.reshape(lanes, length, width)
    arrived_length = arrived_length.reshape(lanes)
    present = arrived_length > 0
    arrived_slot = jnp.cumsum(present.astype(jnp.int32)) - 1
    matches = (arrived_slot[None, :] == local[:, None]) & present[None, :]
    chosen = jnp.sum(jnp.where(matches, lane_ids[None, :], 0), axis=1)
    lengths = jnp.sum(jnp.where(matches, arrived_length[None, :], 0), axis=1)
    moved = arrived if lanes == slots else jnp.take(arrived, chosen, axis=0)
    whole = lax.all_gather(moved, ("tensor", "sub"), axis=2, tiled=True)
    tokens = whole.reshape(slots * length, whole.shape[2]).astype(jnp.float32)
    square_mean = jnp.mean(tokens * tokens, axis=-1, keepdims=True)
    normed_query = (tokens * lax.rsqrt(square_mean + EPS) * in_gain).astype(jnp.bfloat16)
    groups = joined_projection_weight.shape[1]
    head_dim = query_gain.shape[0]
    group_query = joined_projection_weight.shape[2] - 2 * head_dim
    half_heads = group_query // head_dim // lax.axis_size("sub")
    query_cols = half_heads * head_dim
    core = lax.axis_index("sub")
    own_query = lax.dynamic_slice_in_dim(joined_projection_weight, core * query_cols, query_cols, 2)
    extra = joined_projection_weight[:, :, group_query:]
    columns = jnp.concatenate([own_query, extra], axis=2)
    span = columns.shape[2]
    flat_columns = columns.reshape(columns.shape[0], groups * span)
    copies = lax.axis_size("groups")
    rows = flat_columns.shape[0] // copies
    own_rows = lax.dynamic_slice_in_dim(flat_columns, lax.axis_index("groups") * rows, rows, 0)
    mixed_projection = jnp.dot(
        normed_query,
        lax.all_gather(own_rows, ("dp", "groups"), axis=0, tiled=True),
        preferred_element_type=jnp.float32,
    )
    mixed_projection = mixed_projection.reshape(slots, length, groups, span)
    token_positions = jnp.arange(length, dtype=jnp.int32)
    live = token_positions[None, :] < lengths[:, None]
    query_rows = mixed_projection[..., :query_cols].reshape(
        slots, length, groups * half_heads, head_dim
    )
    query_rows = rotary_embed(per_head_norm(query_rows, query_gain), token_positions).astype(
        jnp.bfloat16
    )
    key_rows = rotary_embed(
        per_head_norm(mixed_projection[..., query_cols : query_cols + head_dim], k_gain),
        token_positions,
    )
    key_rows = jnp.where(live[:, :, None, None], key_rows, 0.0).astype(jnp.bfloat16)
    value_rows = jnp.where(
        live[:, :, None, None], mixed_projection[..., query_cols + head_dim :], 0.0
    ).astype(jnp.bfloat16)
    grouped_heads = query_rows.reshape(slots, length, groups, half_heads, head_dim)
    scores = jnp.einsum(
        "nqghd,nkgd->nghqk", grouped_heads, key_rows, preferred_element_type=jnp.float32
    ) * head_dim ** (-0.5)
    causal = token_positions[None, :] <= token_positions[:, None]
    allowed = causal[None, None, None, :, :] & live[:, None, None, None, :]
    weights = jnp.where(allowed, jnp.exp(scores), 0.0)
    probs = (weights / jnp.sum(weights, axis=-1, keepdims=True)).astype(jnp.bfloat16)
    context = jnp.einsum("nghqk,nkgd->nqghd", probs, value_rows, preferred_element_type=jnp.float32)
    context = jnp.where(live[:, :, None, None, None], context, 0.0)
    context = context.reshape(slots, length, groups, half_heads * head_dim).astype(jnp.bfloat16)
    share = length // lax.axis_size("sub")
    key_share = lax.dynamic_slice_in_dim(key_rows, core * share, share, 1).reshape(
        slots, share, groups * head_dim
    )
    value_share = lax.dynamic_slice_in_dim(value_rows, core * share, share, 1).reshape(
        slots, share, groups * head_dim
    )
    return (key_share, value_share, context)


CHUNK = 256


def exchange_kernel(
    tok, lens, w, q_out, kv_out, len_out,
    a, wm, psend, prec, own, ssend, srecv, scales, kvown, kvrecv, lrecv,
    s1s, s1r, s2s, s2r, s3s, s3r, s4s, s4r,
    ws, wr, wfs, wfr, ps, pr, ss, sr, ls, lr, kvs, kvr,
):
    g = lax.axis_index("groups")
    z = lax.axis_index("dp")
    x = lax.axis_index("tensor")
    s = lax.axis_index("sub")
    here = z % 2
    pair = z // 2
    half = w.shape[0] // 2
    n_chunks = wm.shape[0]
    x_mate = (g, z, 1 - x, s)
    sibling = (g, z, x, 1 - s)
    z_mate = (g, pair * 2 + (1 - here), x, s)
    y_mate = (1 - g, z, x, s)
    far = (g, (1 - pair) * 2 + here, x, s)

    barrier = pltpu.get_barrier_semaphore()
    for dz in range(1, 4):
        for dx in range(2):
            pl.semaphore_signal(
                barrier, inc=1, device_id=(g, (z + dz) % 4, (x + dx) % 2, s),
                device_id_type=pl.DeviceIdType.MESH,
            )
    for other in (x_mate, sibling, y_mate):
        pl.semaphore_signal(barrier, inc=1, device_id=other, device_id_type=pl.DeviceIdType.MESH)
    pl.semaphore_wait(barrier, 9)

    def remote(src, dst, send, recv, device):
        return pltpu.make_async_remote_copy(
            src_ref=src, dst_ref=dst, send_sem=send, recv_sem=recv,
            device_id=device, device_id_type=pl.DeviceIdType.MESH,
        )

    def first(o, b, h):
        target = 2 * ((x + 1 + o) % 2) + b
        src = tok.at[target, h]
        dst = a.at[o, s, z, h]
        zt = 2 * x + b
        stays = (zt == z) & (x == h)
        return (
            stays,
            remote(src, dst, s1s.at[o, b, h], s1r.at[o, z], (g, zt, h, s)),
            pltpu.make_async_copy(src, dst, s1r.at[o, z]),
        )

    def start_first(o):
        for b in range(2):
            for h in range(2):
                stays, away, local = first(o, b, h)
                pl.when(jnp.logical_not(stays))(away.start)
                pl.when(stays)(local.start)

    def arrived(o, zs):
        dst = a.at[o, s, zs, x]
        local = (pair == x) & (z == zs)
        pl.when(jnp.logical_not(local))(
            remote(dst, dst, s1s.at[o, 0, 0], s1r.at[o, zs], x_mate).wait_recv
        )
        pl.when(local)(pltpu.make_async_copy(tok.at[0, 0], dst, s1r.at[o, zs]).wait)

    def to_x(o, zs):
        piece = a.at[o, s, zs, x]
        return remote(piece, piece, s2s.at[o, zs], s2r.at[o, zs], x_mate)

    def from_x(o, zs):
        piece = a.at[o, s, zs, 1 - x]
        return remote(piece, piece, s2s.at[o, zs], s2r.at[o, zs], x_mate)

    def to_sub(o, zs):
        piece = a.at[o, s, zs, x]
        return remote(piece, piece, s3s.at[o, zs], s3r.at[o, zs], sibling)

    def from_sub(o, zs):
        piece = a.at[o, 1 - s, zs, x]
        return remote(piece, piece, s3s.at[o, zs], s3r.at[o, zs], sibling)

    def to_sub_late(o, zs):
        piece = a.at[o, s, zs, 1 - x]
        return remote(piece, piece, s4s.at[o, zs], s4r.at[o, zs], sibling)

    def from_sub_late(o, zs):
        piece = a.at[o, 1 - s, zs, 1 - x]
        return remote(piece, piece, s4s.at[o, zs], s4r.at[o, zs], sibling)

    def forward_first(o):
        for zs in range(4):
            arrived(o, zs)
            to_x(o, zs).start()
            to_sub(o, zs).start()

    def forward_second(o):
        for zs in range(4):
            from_x(o, zs).wait_recv()
            to_sub_late(o, zs).start()

    def forward_last(o):
        for zs in range(4):
            from_sub(o, zs).wait_recv()
            from_sub_late(o, zs).wait_recv()

    def w_copy(c):
        rows = pl.ds(pl.multiple_of(g * half, half), half)
        cols = pl.ds(pl.multiple_of(c * CHUNK, CHUNK), CHUNK)
        return remote(w.at[rows, cols], wm.at[c, rows], ws.at[c], wr.at[c], z_mate)

    def w_forward(c):
        rows = pl.ds(pl.multiple_of(g * half, half), half)
        return remote(wm.at[c, rows], wm.at[c, rows], wfs.at[c], wfr.at[c], y_mate)

    def w_forwarded(c):
        rows = pl.ds(pl.multiple_of((1 - g) * half, half), half)
        return remote(wm.at[c, rows], wm.at[c, rows], wfs.at[c], wfr.at[c], y_mate)

    def p_copy(c):
        return remote(psend.at[c], prec.at[c], ps.at[c], pr.at[c], far)

    def s_copy():
        return remote(ssend, srecv, ss.at[0], sr.at[0], far)

    def kv_copy():
        return remote(kvown, kvrecv, kvs.at[0], kvr.at[0], sibling)

    def len_copy(step):
        zt = (z + step) % 4
        return remote(lens.at[zt], lrecv.at[z], ls.at[step], lr.at[step], (g, zt, x, s))

    def product(o, c):
        def tokens(block):
            t = a[o, block]
            return t.reshape(t.shape[0] * t.shape[1] * t.shape[2], t.shape[3])

        cols = pl.ds(pl.multiple_of(c * CHUNK, CHUNK), CHUNK)
        return jnp.dot(
            tokens(here), w[:, cols], preferred_element_type=jnp.float32
        ) + jnp.dot(tokens(1 - here), wm[c], preferred_element_type=jnp.float32)

    def squares(o, zs):
        total = None
        for block in range(2):
            t = a[o, block, zs].reshape(128, a.shape[5]).astype(jnp.float32)
            part = jnp.sum(t * t, axis=1, keepdims=True)
            total = part if total is None else total + part
        return total

    start_first(0)
    for step in range(1, 4):
        len_copy(step).start()
    for c in range(2):
        w_copy(c).start()

    forward_first(0)
    for c in range(2, n_chunks):
        w_copy(c).start()
    start_first(1)
    w_copy(0).wait_recv()
    w_forward(0).start()
    forward_second(0)
    forward_last(0)

    def send_partial(c):
        w_forwarded(c).wait_recv()
        psend[c] = product(0, c).astype(psend.dtype)
        p_copy(c).start()

    @pl.loop(1, n_chunks)
    def _(c):
        w_copy(c).wait_recv()
        w_forward(c).start()
        send_partial(c - 1)
        pl.when(c == n_chunks - 2)(lambda: forward_first(1))
        pl.when(c == n_chunks - 1)(lambda: forward_second(1))

    send_partial(n_chunks - 1)

    @pl.loop(0, 4)
    def _(zs):
        ssend[zs] = jnp.broadcast_to(squares(0, zs), (128, 128)).T[:8]

    s_copy().start()

    forward_last(1)

    @pl.loop(0, n_chunks)
    def _(c):
        own[c] = product(1, c)

    s_copy().wait_recv()

    @pl.loop(0, 4)
    def _(zs):
        rows = pl.ds(pl.multiple_of(zs * 128, 128), 128)
        total = squares(1, zs) + jnp.broadcast_to(srecv[zs, 0:1], (128, 128)).T
        scales[rows, :] = lax.rsqrt(total / (4 * a.shape[5]) + EPS)

    scale = jnp.concatenate([scales[...]] * (CHUNK // 128), axis=1)
    p_copy(0).wait_recv()
    kvown[...] = (own[0] + prec[0].astype(jnp.float32)) * scale
    kv_copy().start()
    kv_out[s] = kvown[...]

    @pl.loop(1, n_chunks)
    def _(c):
        p_copy(c).wait_recv()
        wide = jnp.concatenate([scales[...]] * (CHUNK // 128), axis=1)
        q_out[c - 1] = (own[c] + prec[c].astype(jnp.float32)) * wide

    len_out[z] = lens[z]
    for step in range(1, 4):
        source = (z + 4 - step) % 4
        remote(lrecv.at[source], lrecv.at[source], ls.at[step], lr.at[step], x_mate).wait_recv()
        len_out[source] = lrecv[source]

    kv_copy().wait_recv()
    kv_out[1 - s] = kvrecv[...]

    for o in range(2):
        for b in range(2):
            for h in range(2):
                stays, away, _ = first(o, b, h)
                pl.when(jnp.logical_not(stays))(away.wait_send)
        for zs in range(4):
            to_x(o, zs).wait_send()
            to_sub(o, zs).wait_send()
            to_sub_late(o, zs).wait_send()
    for c in range(n_chunks):
        w_copy(c).wait_send()
        w_forward(c).wait_send()
        p_copy(c).wait_send()
    s_copy().wait_send()
    kv_copy().wait_send()
    for step in range(1, 4):
        len_copy(step).wait_send()


def exchange(tok, lens, w):
    width = w.shape[0]
    columns = CHUNK
    chunks = w.shape[1] // columns
    tokens = tok.shape[0] * tok.shape[1] * tok.shape[2]
    dma = pltpu.SemaphoreType.DMA
    vmem = pl.BlockSpec(memory_space=pltpu.VMEM)
    f32 = jnp.float32
    bf16 = jnp.bfloat16
    return pl.pallas_call(
        exchange_kernel,
        out_shape=(
            jax.ShapeDtypeStruct((chunks - 1, tokens, columns), f32),
            jax.ShapeDtypeStruct((2, tokens, columns), f32),
            jax.ShapeDtypeStruct(lens.shape, f32),
        ),
        in_specs=[pl.BlockSpec(memory_space=pl.ANY), vmem, vmem],
        out_specs=(vmem, vmem, vmem),
        scratch_shapes=[
            pltpu.VMEM((2, 2, 4, 2, tok.shape[2], width), bf16),
            pltpu.VMEM((chunks, width, columns), bf16),
            pltpu.VMEM((chunks, tokens, columns), bf16),
            pltpu.VMEM((chunks, tokens, columns), bf16),
            pltpu.VMEM((chunks, tokens, columns), f32),
            pltpu.VMEM(lens.shape, f32),
            pltpu.VMEM(lens.shape, f32),
            pltpu.VMEM((tokens, 128), f32),
            pltpu.VMEM((tokens, columns), f32),
            pltpu.VMEM((tokens, columns), f32),
            pltpu.VMEM(lens.shape, f32),
            dma((2, 2, 2)), dma((2, 4)), dma((2, 4)), dma((2, 4)),
            dma((2, 4)), dma((2, 4)), dma((2, 4)), dma((2, 4)),
            dma((chunks,)), dma((chunks,)), dma((chunks,)), dma((chunks,)),
            dma((chunks,)), dma((chunks,)), dma((1,)), dma((1,)),
            dma((4,)), dma((4,)), dma((1,)), dma((1,)),
        ],
        compiler_params=pltpu.CompilerParams(
            collective_id=0, has_side_effects=True, vmem_limit_bytes=48 << 20
        ),
        cost_estimate=pl.CostEstimate(
            flops=8 * tokens * width * chunks * columns, bytes_accessed=1 << 24, transcendentals=0
        ),
        name="exchange",
    )(tok, lens, w)


def attend_kernel(q_ref, kv_ref, len_ref, cos_ref, sin_ref, qg_ref, kg_ref, k_out, v_out, ctx_out):
    head = cos_ref.shape[1]
    rows = cos_ref.shape[0]
    seqs, share, _ = k_out.shape
    length = rows // seqs
    core = lax.axis_index("sub")
    len_key = jnp.broadcast_to(len_ref[0, 0:1, :], (rows, rows))
    len_query = len_key.T
    row_ids = lax.broadcasted_iota(jnp.int32, (rows, rows), 0)
    col_ids = lax.broadcasted_iota(jnp.int32, (rows, rows), 1)
    key_pos = (col_ids % length).astype(jnp.float32)
    query_pos = (row_ids % length).astype(jnp.float32)
    allowed = (
        (row_ids // length == col_ids // length) & (col_ids <= row_ids) & (key_pos < len_key)
    )
    live = query_pos < len_query
    cos = cos_ref[...]
    sin = sin_ref[...]

    def norm_rope(t, gain):
        mean = jnp.mean(t * t, axis=-1, keepdims=True)
        t = t * lax.rsqrt(mean + EPS) * gain
        return t * cos + pltpu.roll(t, head // 2, 1) * sin

    def part(t):
        t = t.reshape(seqs, length, head)
        return jnp.where(core == 0, t[:, :share], t[:, share:])

    kgain = kg_ref[...]
    qgain = qg_ref[...]
    n_groups = kv_ref.shape[2] // head
    heads = q_ref.shape[0] * q_ref.shape[2] // head // n_groups
    per_chunk = q_ref.shape[2] // head
    for group in range(n_groups):
        cols = slice(group * head, (group + 1) * head)
        key = jnp.where(live, norm_rope(kv_ref[0, :, cols], kgain), 0.0)
        value = jnp.where(live, kv_ref[1, :, cols], 0.0)
        k_out[:, :, cols] = part(key).astype(k_out.dtype)
        v_out[:, :, cols] = part(value).astype(v_out.dtype)
        key = key.astype(jnp.bfloat16)
        value = value.astype(jnp.bfloat16)
        for h in range(heads):
            n = group * heads + h
            at = n % per_chunk * head
            query = norm_rope(q_ref[n // per_chunk, :, at : at + head], qgain)
            scores = lax.dot_general(
                query.astype(jnp.bfloat16), key, (((1,), (1,)), ((), ())),
                preferred_element_type=jnp.float32,
            ) * head ** (-0.5)
            weights = jnp.where(allowed, jnp.exp(scores), 0.0)
            probs = weights / jnp.sum(weights, axis=-1, keepdims=True)
            out = jnp.dot(probs.astype(jnp.bfloat16), value, preferred_element_type=jnp.float32)
            ctx_out[:, n * head : (n + 1) * head] = jnp.where(live, out, 0.0).astype(ctx_out.dtype)


def attend(q, kv, lens, query_gain, k_gain, length, share):
    head = query_gain.shape[0]
    chunks, tokens, columns = q.shape
    blocks = lens.shape[0]
    rows = tokens // blocks
    seqs = rows // length
    frequency = THETA ** (-(2.0 * jnp.arange(head // 2, dtype=jnp.float32)) / head)
    positions = jnp.arange(rows, dtype=jnp.int32) % length
    angle = positions.astype(jnp.float32)[:, None] * frequency[None, :]
    cos = jnp.cos(angle)
    sin = jnp.sin(angle)
    whole = lambda *shape: pl.BlockSpec(shape, lambda i: (0,) * len(shape))
    cache = jax.ShapeDtypeStruct((tokens // length, share, columns), jnp.bfloat16)
    return pl.pallas_call(
        attend_kernel,
        grid=(blocks,),
        out_shape=(cache, cache, jax.ShapeDtypeStruct((tokens, chunks * columns), jnp.bfloat16)),
        in_specs=[
            pl.BlockSpec((chunks, rows, columns), lambda i: (0, i, 0)),
            pl.BlockSpec((2, rows, columns), lambda i: (0, i, 0)),
            pl.BlockSpec((1,) + lens.shape[1:], lambda i: (i, 0, 0)),
            whole(rows, head), whole(rows, head), whole(1, head), whole(1, head),
        ],
        out_specs=(
            pl.BlockSpec((seqs, share, columns), lambda i: (i, 0, 0)),
            pl.BlockSpec((seqs, share, columns), lambda i: (i, 0, 0)),
            pl.BlockSpec((rows, chunks * columns), lambda i: (i, 0)),
        ),
        compiler_params=pltpu.CompilerParams(vmem_limit_bytes=32 << 20),
        name="attend",
    )(
        q, kv, lens,
        jnp.concatenate([cos, cos], axis=1), jnp.concatenate([-sin, sin], axis=1),
        query_gain[None, :], k_gain[None, :],
    )


def paired_body(
    hidden, seq_len, target_rank, in_gain, joined_projection_weight, query_gain, k_gain
):
    slots, length, width = hidden.shape
    ranks = lax.axis_size("dp")
    pair = slots // ranks
    local = jnp.arange(slots, dtype=jnp.int32)
    same_target = (target_rank[:, None] == target_rank[None, :]) & (local[None, :] < local[:, None])
    position = target_rank * pair + jnp.sum(same_target.astype(jnp.int32), axis=1)
    hits = local[:, None] == position[None, :]
    source = jnp.sum(jnp.where(hits, local[None, :], 0), axis=1)
    sent_length = jnp.sum(jnp.where(hits, seq_len[None, :], 0), axis=1)
    tok = jnp.take(hidden, source, axis=0, mode="clip").reshape(ranks, 2, pair // 2 * length, width)
    lens = jnp.broadcast_to(
        sent_length.astype(jnp.float32).reshape(ranks, 1, pair, 1), (ranks, 8, pair, length)
    ).reshape(ranks, 8, pair * length)

    head = query_gain.shape[0]
    rows, groups, span = joined_projection_weight.shape
    group_query = span - 2 * head
    query_cols = group_query // lax.axis_size("sub")
    core = lax.axis_index("sub")
    gain = lax.dynamic_slice_in_dim(in_gain, lax.axis_index("dp") * rows, rows, 0)
    own_query = lax.dynamic_slice_in_dim(joined_projection_weight, core * query_cols, query_cols, 2)
    own_kv = lax.dynamic_slice_in_dim(
        joined_projection_weight, group_query + core * head, head, 2
    )
    columns = [own_kv[:, i] for i in range(groups)] + [own_query[:, i] for i in range(groups)]
    flat = jnp.concatenate(columns, axis=1).astype(jnp.float32) * gain[:, None]
    w = flat.astype(jnp.bfloat16)

    q, kv, lengths = exchange(tok, lens, w)
    share = length // lax.axis_size("sub")
    key_share, value_share, context = attend(q, kv, lengths, query_gain, k_gain, length, share)
    return (key_share, value_share, context.reshape(slots, length, groups, query_cols))


def solution(mesh):
    sizes = mesh.shape
    paired = (
        sizes["dp"] == 4 and sizes["tensor"] == 2 and sizes["sub"] == 2 and sizes["groups"] == 2
    )
    placed = (
        P(("groups", "dp"), None, ("tensor", "sub")),
        P(("groups", "dp")),
        P(("groups", "dp")),
        P(),
        P("dp", "tensor", None),
        P(),
        P(),
    )
    return jax.shard_map(
        paired_body if paired else body,
        mesh=mesh,
        in_specs=placed,
        out_specs=(
            P(("groups", "dp"), "sub", "tensor"),
            P(("groups", "dp"), "sub", "tensor"),
            P(("groups", "dp"), None, "tensor", "sub"),
        ),
        check_vma=False,
    )
```

```python
import functools

import jax
import jax.numpy as jnp
from jax import lax
from jax.experimental import pallas as pl
from jax.experimental.pallas import tpu as pltpu
from jax.sharding import PartitionSpec as P

EPS = 1e-06
THETA = 1000000.0


def per_head_norm(value_rows, gain):
    square_mean = jnp.mean(value_rows * value_rows, axis=-1, keepdims=True)
    return value_rows * lax.rsqrt(square_mean + EPS) * gain


def rotary_embed(value_rows, token_positions):
    half_width = value_rows.shape[-1] // 2
    frequency = THETA ** (-(2.0 * jnp.arange(half_width, dtype=jnp.float32)) / value_rows.shape[-1])
    angle = token_positions.astype(jnp.float32)[:, None] * frequency[None, :]
    cosine = jnp.cos(angle)[None, :, None, :]
    sine = jnp.sin(angle)[None, :, None, :]
    first = value_rows[..., :half_width]
    second = value_rows[..., half_width:]
    return jnp.concatenate(
        [first * cosine - second * sine, second * cosine + first * sine], axis=-1
    )


def body(hidden, seq_len, target_rank, in_gain, joined_projection_weight, query_gain, k_gain):
    slots, length, width = hidden.shape
    ranks = lax.axis_size("dp")
    pair = -(-slots // ranks)
    lanes = ranks * pair
    local = jnp.arange(slots, dtype=jnp.int32)
    same_target = (target_rank[:, None] == target_rank[None, :]) & (local[None, :] < local[:, None])
    earlier = jnp.sum(same_target.astype(jnp.int32), axis=1)
    position = target_rank * pair + earlier
    lane_ids = jnp.arange(lanes, dtype=jnp.int32)
    hits = lane_ids[:, None] == position[None, :]
    filled = jnp.any(hits, axis=1)
    source = jnp.sum(jnp.where(hits, local[None, :], 0), axis=1)
    outgoing = jnp.where(
        filled[:, None, None], jnp.take(hidden, source, axis=0), jnp.zeros((), hidden.dtype)
    )
    sent_length = jnp.where(filled, jnp.take(seq_len, source), 0)
    arrived, arrived_length = (
        lax.all_to_all(
            outgoing.reshape(ranks, pair, length, width),
            "dp",
            split_axis=0,
            concat_axis=0,
            tiled=True,
        ),
        lax.all_to_all(
            sent_length.reshape(ranks, pair), "dp", split_axis=0, concat_axis=0, tiled=True
        ),
    )
    arrived = arrived.reshape(lanes, length, width)
    arrived_length = arrived_length.reshape(lanes)
    present = arrived_length > 0
    arrived_slot = jnp.cumsum(present.astype(jnp.int32)) - 1
    matches = (arrived_slot[None, :] == local[:, None]) & present[None, :]
    chosen = jnp.sum(jnp.where(matches, lane_ids[None, :], 0), axis=1)
    lengths = jnp.sum(jnp.where(matches, arrived_length[None, :], 0), axis=1)
    moved = arrived if lanes == slots else jnp.take(arrived, chosen, axis=0)
    whole = lax.all_gather(moved, ("tensor", "sub"), axis=2, tiled=True)
    tokens = whole.reshape(slots * length, whole.shape[2]).astype(jnp.float32)
    square_mean = jnp.mean(tokens * tokens, axis=-1, keepdims=True)
    normed_query = (tokens * lax.rsqrt(square_mean + EPS) * in_gain).astype(jnp.bfloat16)
    groups = joined_projection_weight.shape[1]
    head_dim = query_gain.shape[0]
    group_query = joined_projection_weight.shape[2] - 2 * head_dim
    half_heads = group_query // head_dim // lax.axis_size("sub")
    query_cols = half_heads * head_dim
    core = lax.axis_index("sub")
    own_query = lax.dynamic_slice_in_dim(joined_projection_weight, core * query_cols, query_cols, 2)
    extra = joined_projection_weight[:, :, group_query:]
    columns = jnp.concatenate([own_query, extra], axis=2)
    span = columns.shape[2]
    flat_columns = columns.reshape(columns.shape[0], groups * span)
    copies = lax.axis_size("groups")
    rows = flat_columns.shape[0] // copies
    own_rows = lax.dynamic_slice_in_dim(flat_columns, lax.axis_index("groups") * rows, rows, 0)
    mixed_projection = jnp.dot(
        normed_query,
        lax.all_gather(own_rows, ("dp", "groups"), axis=0, tiled=True),
        preferred_element_type=jnp.float32,
    )
    mixed_projection = mixed_projection.reshape(slots, length, groups, span)
    token_positions = jnp.arange(length, dtype=jnp.int32)
    live = token_positions[None, :] < lengths[:, None]
    query_rows = mixed_projection[..., :query_cols].reshape(
        slots, length, groups * half_heads, head_dim
    )
    query_rows = rotary_embed(per_head_norm(query_rows, query_gain), token_positions).astype(
        jnp.bfloat16
    )
    key_rows = rotary_embed(
        per_head_norm(mixed_projection[..., query_cols : query_cols + head_dim], k_gain),
        token_positions,
    )
    key_rows = jnp.where(live[:, :, None, None], key_rows, 0.0).astype(jnp.bfloat16)
    value_rows = jnp.where(
        live[:, :, None, None], mixed_projection[..., query_cols + head_dim :], 0.0
    ).astype(jnp.bfloat16)
    grouped_heads = query_rows.reshape(slots, length, groups, half_heads, head_dim)
    scores = jnp.einsum(
        "nqghd,nkgd->nghqk", grouped_heads, key_rows, preferred_element_type=jnp.float32
    ) * head_dim ** (-0.5)
    causal = token_positions[None, :] <= token_positions[:, None]
    allowed = causal[None, None, None, :, :] & live[:, None, None, None, :]
    weights = jnp.where(allowed, jnp.exp(scores), 0.0)
    probs = (weights / jnp.sum(weights, axis=-1, keepdims=True)).astype(jnp.bfloat16)
    context = jnp.einsum("nghqk,nkgd->nqghd", probs, value_rows, preferred_element_type=jnp.float32)
    context = jnp.where(live[:, :, None, None, None], context, 0.0)
    context = context.reshape(slots, length, groups, half_heads * head_dim).astype(jnp.bfloat16)
    share = length // lax.axis_size("sub")
    key_share = lax.dynamic_slice_in_dim(key_rows, core * share, share, 1).reshape(
        slots, share, groups * head_dim
    )
    value_share = lax.dynamic_slice_in_dim(value_rows, core * share, share, 1).reshape(
        slots, share, groups * head_dim
    )
    return (key_share, value_share, context)


CHUNK = 256


def exchange_kernel(
    tok, lens, w, q_out, kv_out, len_out,
    a, wm, psend, prec, own, ssend, srecv, scales, kvown, kvrecv, lrecv, relay,
    rs, rr, fs,
    s1s, s1r, s2s, s2r, s3s, s3r, s4s, s4r,
    ws, wr, wfs, wfr, ps, pr, ss, sr, ls, lr, kvs, kvr,
):
    g = lax.axis_index("groups")
    z = lax.axis_index("dp")
    x = lax.axis_index("tensor")
    s = lax.axis_index("sub")
    here = z % 2
    pair = z // 2
    half = w.shape[0] // 2
    n_chunks = wm.shape[0]
    x_mate = (g, z, 1 - x, s)
    sibling = (g, z, x, 1 - s)
    z_mate = (g, pair * 2 + (1 - here), x, s)
    y_mate = (1 - g, z, x, s)
    far = (g, (1 - pair) * 2 + here, x, s)

    barrier = pltpu.get_barrier_semaphore()
    for dz in range(1, 4):
        for dx in range(2):
            pl.semaphore_signal(
                barrier, inc=1, device_id=(g, (z + dz) % 4, (x + dx) % 2, s),
                device_id_type=pl.DeviceIdType.MESH,
            )
    for other in (x_mate, sibling, y_mate):
        pl.semaphore_signal(barrier, inc=1, device_id=other, device_id_type=pl.DeviceIdType.MESH)
    pl.semaphore_wait(barrier, 9)

    def remote(src, dst, send, recv, device):
        return pltpu.make_async_remote_copy(
            src_ref=src, dst_ref=dst, send_sem=send, recv_sem=recv,
            device_id=device, device_id_type=pl.DeviceIdType.MESH,
        )

    def first(o, b):
        target = 2 * ((x + 1 + o) % 2) + b
        zt = 2 * x + b
        near, across = tok.at[target, x], tok.at[target, 1 - x]
        return (
            zt == z,
            remote(near, a.at[o, s, z, x], s1s.at[o, b, 0], s1r.at[o, z], (g, zt, x, s)),
            pltpu.make_async_copy(near, a.at[o, s, z, x], s1r.at[o, z]),
            remote(across, a.at[o, s, z, 1 - x], s1s.at[o, b, 1], s1r.at[o, z], x_mate),
            remote(across, relay.at[o, b], rs.at[o, b], rr.at[o, b], x_mate),
        )

    def start_first(o):
        for b in range(2):
            stays, away, local, beside, over = first(o, b)
            pl.when(jnp.logical_not(stays))(over.start)
            pl.when(stays)(beside.start)
            pl.when(jnp.logical_not(stays))(away.start)
            pl.when(stays)(local.start)

    def onward(o, b):
        zt = 2 * (1 - x) + b
        return zt != z, remote(
            relay.at[o, b], a.at[o, s, z, x], fs.at[o, b], s1r.at[o, z], (g, zt, x, s)
        )

    def pass_on(o):
        for b in range(2):
            leaves, copy = onward(o, b)

            @pl.when(leaves)
            def _():
                remote(relay.at[o, b], relay.at[o, b], rs.at[o, b], rr.at[o, b], x_mate).wait_recv()
                copy.start()

    def arrived(o, zs):
        dst = a.at[o, s, zs, x]
        local = (pair == x) & (z == zs)
        pl.when(jnp.logical_not(local))(
            remote(dst, dst, s1s.at[o, 0, 0], s1r.at[o, zs], x_mate).wait_recv
        )
        pl.when(local)(pltpu.make_async_copy(tok.at[0, 0], dst, s1r.at[o, zs]).wait)

    def to_x(o, zs):
        piece = a.at[o, s, zs, x]
        return remote(piece, piece, s2s.at[o, zs], s2r.at[o, zs], x_mate)

    def from_x(o, zs):
        piece = a.at[o, s, zs, 1 - x]
        return remote(piece, piece, s2s.at[o, zs], s2r.at[o, zs], x_mate)

    def to_sub(o, zs):
        piece = a.at[o, s, zs, x]
        return remote(piece, piece, s3s.at[o, zs], s3r.at[o, zs], sibling)

    def from_sub(o, zs):
        piece = a.at[o, 1 - s, zs, x]
        return remote(piece, piece, s3s.at[o, zs], s3r.at[o, zs], sibling)

    def to_sub_late(o, zs):
        piece = a.at[o, s, zs, 1 - x]
        return remote(piece, piece, s4s.at[o, zs], s4r.at[o, zs], sibling)

    def from_sub_late(o, zs):
        piece = a.at[o, 1 - s, zs, 1 - x]
        return remote(piece, piece, s4s.at[o, zs], s4r.at[o, zs], sibling)

    def forward_first(o):
        for zs in range(4):
            arrived(o, zs)
            to_x(o, zs).start()
            to_sub(o, zs).start()

    def forward_second(o):
        for zs in range(4):
            from_x(o, zs).wait_recv()
            to_sub_late(o, zs).start()

    def forward_last(o):
        for zs in range(4):
            from_sub(o, zs).wait_recv()
            from_sub_late(o, zs).wait_recv()

    def w_copy(c):
        rows = pl.ds(pl.multiple_of(g * half, half), half)
        cols = pl.ds(pl.multiple_of(c * CHUNK, CHUNK), CHUNK)
        return remote(w.at[rows, cols], wm.at[c, rows], ws.at[c], wr.at[c], z_mate)

    def w_forward(c):
        rows = pl.ds(pl.multiple_of(g * half, half), half)
        return remote(wm.at[c, rows], wm.at[c, rows], wfs.at[c], wfr.at[c], y_mate)

    def w_forwarded(c):
        rows = pl.ds(pl.multiple_of((1 - g) * half, half), half)
        return remote(wm.at[c, rows], wm.at[c, rows], wfs.at[c], wfr.at[c], y_mate)

    def p_copy(c):
        return remote(psend.at[c], prec.at[c], ps.at[c], pr.at[c], far)

    def s_copy():
        return remote(ssend, srecv, ss.at[0], sr.at[0], far)

    def kv_copy():
        return remote(kvown, kvrecv, kvs.at[0], kvr.at[0], sibling)

    def len_copy(step):
        zt = (z + step) % 4
        return remote(lens.at[zt], lrecv.at[z], ls.at[step], lr.at[step], (g, zt, x, s))

    def product(o, c):
        def tokens(block):
            t = a[o, block]
            return t.reshape(t.shape[0] * t.shape[1] * t.shape[2], t.shape[3])

        cols = pl.ds(pl.multiple_of(c * CHUNK, CHUNK), CHUNK)
        return jnp.dot(
            tokens(here), w[:, cols], preferred_element_type=jnp.float32
        ) + jnp.dot(tokens(1 - here), wm[c], preferred_element_type=jnp.float32)

    def squares(o, zs):
        total = None
        for block in range(2):
            t = a[o, block, zs].reshape(128, a.shape[5]).astype(jnp.float32)
            part = jnp.sum(t * t, axis=1, keepdims=True)
            total = part if total is None else total + part
        return total

    start_first(0)
    for step in range(1, 4):
        len_copy(step).start()
    for c in range(2):
        w_copy(c).start()

    pass_on(0)
    forward_first(0)
    for c in range(2, n_chunks):
        w_copy(c).start()
    start_first(1)
    w_copy(0).wait_recv()
    w_forward(0).start()
    pass_on(1)
    forward_second(0)
    forward_last(0)

    def send_partial(c):
        w_forwarded(c).wait_recv()
        psend[c] = product(0, c).astype(psend.dtype)
        p_copy(c).start()

    @pl.loop(1, n_chunks)
    def _(c):
        w_copy(c).wait_recv()
        w_forward(c).start()
        send_partial(c - 1)
        pl.when(c == n_chunks - 2)(lambda: forward_first(1))
        pl.when(c == n_chunks - 1)(lambda: forward_second(1))

    send_partial(n_chunks - 1)

    @pl.loop(0, 4)
    def _(zs):
        ssend[zs] = jnp.broadcast_to(squares(0, zs), (128, 128)).T[:8]

    s_copy().start()

    forward_last(1)

    @pl.loop(0, n_chunks)
    def _(c):
        own[c] = product(1, c)

    s_copy().wait_recv()

    @pl.loop(0, 4)
    def _(zs):
        rows = pl.ds(pl.multiple_of(zs * 128, 128), 128)
        total = squares(1, zs) + jnp.broadcast_to(srecv[zs, 0:1], (128, 128)).T
        scales[rows, :] = lax.rsqrt(total / (4 * a.shape[5]) + EPS)

    scale = jnp.concatenate([scales[...]] * (CHUNK // 128), axis=1)
    p_copy(0).wait_recv()
    kvown[...] = (own[0] + prec[0].astype(jnp.float32)) * scale
    kv_copy().start()
    kv_out[s] = kvown[...]

    @pl.loop(1, n_chunks)
    def _(c):
        p_copy(c).wait_recv()
        wide = jnp.concatenate([scales[...]] * (CHUNK // 128), axis=1)
        q_out[c - 1] = (own[c] + prec[c].astype(jnp.float32)) * wide

    len_out[z] = lens[z]
    for step in range(1, 4):
        source = (z + 4 - step) % 4
        remote(lrecv.at[source], lrecv.at[source], ls.at[step], lr.at[step], x_mate).wait_recv()
        len_out[source] = lrecv[source]

    kv_copy().wait_recv()
    kv_out[1 - s] = kvrecv[...]

    for o in range(2):
        for b in range(2):
            stays, away, _, beside, over = first(o, b)
            pl.when(jnp.logical_not(stays))(over.wait_send)
            pl.when(stays)(beside.wait_send)
            pl.when(jnp.logical_not(stays))(away.wait_send)
            leaves, copy = onward(o, b)
            pl.when(leaves)(copy.wait_send)
        for zs in range(4):
            to_x(o, zs).wait_send()
            to_sub(o, zs).wait_send()
            to_sub_late(o, zs).wait_send()
    for c in range(n_chunks):
        w_copy(c).wait_send()
        w_forward(c).wait_send()
        p_copy(c).wait_send()
    s_copy().wait_send()
    kv_copy().wait_send()
    for step in range(1, 4):
        len_copy(step).wait_send()


def exchange(tok, lens, w):
    width = w.shape[0]
    columns = CHUNK
    chunks = w.shape[1] // columns
    tokens = tok.shape[0] * tok.shape[1] * tok.shape[2]
    dma = pltpu.SemaphoreType.DMA
    vmem = pl.BlockSpec(memory_space=pltpu.VMEM)
    f32 = jnp.float32
    bf16 = jnp.bfloat16
    return pl.pallas_call(
        exchange_kernel,
        out_shape=(
            jax.ShapeDtypeStruct((chunks - 1, tokens, columns), f32),
            jax.ShapeDtypeStruct((2, tokens, columns), f32),
            jax.ShapeDtypeStruct(lens.shape, f32),
        ),
        in_specs=[pl.BlockSpec(memory_space=pl.ANY), vmem, vmem],
        out_specs=(vmem, vmem, vmem),
        scratch_shapes=[
            pltpu.VMEM((2, 2, 4, 2, tok.shape[2], width), bf16),
            pltpu.VMEM((chunks, width, columns), bf16),
            pltpu.VMEM((chunks, tokens, columns), bf16),
            pltpu.VMEM((chunks, tokens, columns), bf16),
            pltpu.VMEM((chunks, tokens, columns), f32),
            pltpu.VMEM(lens.shape, f32),
            pltpu.VMEM(lens.shape, f32),
            pltpu.VMEM((tokens, 128), f32),
            pltpu.VMEM((tokens, columns), f32),
            pltpu.VMEM((tokens, columns), f32),
            pltpu.VMEM(lens.shape, f32),
            pltpu.VMEM((2, 2, tok.shape[2], width), bf16),
            dma((2, 2)), dma((2, 2)), dma((2, 2)),
            dma((2, 2, 2)), dma((2, 4)), dma((2, 4)), dma((2, 4)),
            dma((2, 4)), dma((2, 4)), dma((2, 4)), dma((2, 4)),
            dma((chunks,)), dma((chunks,)), dma((chunks,)), dma((chunks,)),
            dma((chunks,)), dma((chunks,)), dma((1,)), dma((1,)),
            dma((4,)), dma((4,)), dma((1,)), dma((1,)),
        ],
        compiler_params=pltpu.CompilerParams(
            collective_id=0, has_side_effects=True, vmem_limit_bytes=48 << 20
        ),
        cost_estimate=pl.CostEstimate(
            flops=8 * tokens * width * chunks * columns, bytes_accessed=1 << 24, transcendentals=0
        ),
        name="exchange",
    )(tok, lens, w)


def attend_kernel(q_ref, kv_ref, len_ref, cos_ref, sin_ref, qg_ref, kg_ref, k_out, v_out, ctx_out):
    head = cos_ref.shape[1]
    rows = cos_ref.shape[0]
    seqs, share, _ = k_out.shape
    length = rows // seqs
    core = lax.axis_index("sub")
    len_key = jnp.broadcast_to(len_ref[0, 0:1, :], (rows, rows))
    len_query = len_key.T
    row_ids = lax.broadcasted_iota(jnp.int32, (rows, rows), 0)
    col_ids = lax.broadcasted_iota(jnp.int32, (rows, rows), 1)
    key_pos = (col_ids % length).astype(jnp.float32)
    query_pos = (row_ids % length).astype(jnp.float32)
    allowed = (
        (row_ids // length == col_ids // length) & (col_ids <= row_ids) & (key_pos < len_key)
    )
    live = query_pos < len_query
    cos = cos_ref[...]
    sin = sin_ref[...]

    def norm_rope(t, gain):
        mean = jnp.mean(t * t, axis=-1, keepdims=True)
        t = t * lax.rsqrt(mean + EPS) * gain
        return t * cos + pltpu.roll(t, head // 2, 1) * sin

    def part(t):
        t = t.reshape(seqs, length, head)
        return jnp.where(core == 0, t[:, :share], t[:, share:])

    kgain = kg_ref[...]
    qgain = qg_ref[...]
    n_groups = kv_ref.shape[2] // head
    heads = q_ref.shape[0] * q_ref.shape[2] // head // n_groups
    per_chunk = q_ref.shape[2] // head
    for group in range(n_groups):
        cols = slice(group * head, (group + 1) * head)
        key = jnp.where(live, norm_rope(kv_ref[0, :, cols], kgain), 0.0)
        value = jnp.where(live, kv_ref[1, :, cols], 0.0)
        k_out[:, :, cols] = part(key).astype(k_out.dtype)
        v_out[:, :, cols] = part(value).astype(v_out.dtype)
        key = key.astype(jnp.bfloat16)
        value = value.astype(jnp.bfloat16)
        for h in range(heads):
            n = group * heads + h
            at = n % per_chunk * head
            query = norm_rope(q_ref[n // per_chunk, :, at : at + head], qgain)
            scores = lax.dot_general(
                query.astype(jnp.bfloat16), key, (((1,), (1,)), ((), ())),
                preferred_element_type=jnp.float32,
            ) * head ** (-0.5)
            weights = jnp.where(allowed, jnp.exp(scores), 0.0)
            probs = weights / jnp.sum(weights, axis=-1, keepdims=True)
            out = jnp.dot(probs.astype(jnp.bfloat16), value, preferred_element_type=jnp.float32)
            ctx_out[:, n * head : (n + 1) * head] = jnp.where(live, out, 0.0).astype(ctx_out.dtype)


def attend(q, kv, lens, query_gain, k_gain, length, share):
    head = query_gain.shape[0]
    chunks, tokens, columns = q.shape
    blocks = lens.shape[0]
    rows = tokens // blocks
    seqs = rows // length
    frequency = THETA ** (-(2.0 * jnp.arange(head // 2, dtype=jnp.float32)) / head)
    positions = jnp.arange(rows, dtype=jnp.int32) % length
    angle = positions.astype(jnp.float32)[:, None] * frequency[None, :]
    cos = jnp.cos(angle)
    sin = jnp.sin(angle)
    whole = lambda *shape: pl.BlockSpec(shape, lambda i: (0,) * len(shape))
    cache = jax.ShapeDtypeStruct((tokens // length, share, columns), jnp.bfloat16)
    return pl.pallas_call(
        attend_kernel,
        grid=(blocks,),
        out_shape=(cache, cache, jax.ShapeDtypeStruct((tokens, chunks * columns), jnp.bfloat16)),
        in_specs=[
            pl.BlockSpec((chunks, rows, columns), lambda i: (0, i, 0)),
            pl.BlockSpec((2, rows, columns), lambda i: (0, i, 0)),
            pl.BlockSpec((1,) + lens.shape[1:], lambda i: (i, 0, 0)),
            whole(rows, head), whole(rows, head), whole(1, head), whole(1, head),
        ],
        out_specs=(
            pl.BlockSpec((seqs, share, columns), lambda i: (i, 0, 0)),
            pl.BlockSpec((seqs, share, columns), lambda i: (i, 0, 0)),
            pl.BlockSpec((rows, chunks * columns), lambda i: (i, 0)),
        ),
        compiler_params=pltpu.CompilerParams(vmem_limit_bytes=32 << 20),
        name="attend",
    )(
        q, kv, lens,
        jnp.concatenate([cos, cos], axis=1), jnp.concatenate([-sin, sin], axis=1),
        query_gain[None, :], k_gain[None, :],
    )


def paired_body(
    hidden, seq_len, target_rank, in_gain, joined_projection_weight, query_gain, k_gain
):
    slots, length, width = hidden.shape
    ranks = lax.axis_size("dp")
    pair = slots // ranks
    local = jnp.arange(slots, dtype=jnp.int32)
    same_target = (target_rank[:, None] == target_rank[None, :]) & (local[None, :] < local[:, None])
    position = target_rank * pair + jnp.sum(same_target.astype(jnp.int32), axis=1)
    hits = local[:, None] == position[None, :]
    source = jnp.sum(jnp.where(hits, local[None, :], 0), axis=1)
    sent_length = jnp.sum(jnp.where(hits, seq_len[None, :], 0), axis=1)
    tok = jnp.take(hidden, source, axis=0, mode="clip").reshape(ranks, 2, pair // 2 * length, width)
    lens = jnp.broadcast_to(
        sent_length.astype(jnp.float32).reshape(ranks, 1, pair, 1), (ranks, 8, pair, length)
    ).reshape(ranks, 8, pair * length)

    head = query_gain.shape[0]
    rows, groups, span = joined_projection_weight.shape
    group_query = span - 2 * head
    query_cols = group_query // lax.axis_size("sub")
    core = lax.axis_index("sub")
    gain = lax.dynamic_slice_in_dim(in_gain, lax.axis_index("dp") * rows, rows, 0)
    own_query = lax.dynamic_slice_in_dim(joined_projection_weight, core * query_cols, query_cols, 2)
    own_kv = lax.dynamic_slice_in_dim(
        joined_projection_weight, group_query + core * head, head, 2
    )
    columns = [own_kv[:, i] for i in range(groups)] + [own_query[:, i] for i in range(groups)]
    flat = jnp.concatenate(columns, axis=1).astype(jnp.float32) * gain[:, None]
    w = flat.astype(jnp.bfloat16)

    q, kv, lengths = exchange(tok, lens, w)
    share = length // lax.axis_size("sub")
    key_share, value_share, context = attend(q, kv, lengths, query_gain, k_gain, length, share)
    return (key_share, value_share, context.reshape(slots, length, groups, query_cols))


def solution(mesh):
    sizes = mesh.shape
    paired = (
        sizes["dp"] == 4 and sizes["tensor"] == 2 and sizes["sub"] == 2 and sizes["groups"] == 2
    )
    placed = (
        P(("groups", "dp"), None, ("tensor", "sub")),
        P(("groups", "dp")),
        P(("groups", "dp")),
        P(),
        P("dp", "tensor", None),
        P(),
        P(),
    )
    return jax.shard_map(
        paired_body if paired else body,
        mesh=mesh,
        in_specs=placed,
        out_specs=(
            P(("groups", "dp"), "sub", "tensor"),
            P(("groups", "dp"), "sub", "tensor"),
            P(("groups", "dp"), None, "tensor", "sub"),
        ),
        check_vma=False,
    )
```

```python
import functools

import jax
import jax.numpy as jnp
from jax import lax
from jax.experimental import pallas as pl
from jax.experimental.pallas import tpu as pltpu
from jax.sharding import PartitionSpec as P

EPS = 1e-06
THETA = 1000000.0


def per_head_norm(value_rows, gain):
    square_mean = jnp.mean(value_rows * value_rows, axis=-1, keepdims=True)
    return value_rows * lax.rsqrt(square_mean + EPS) * gain


def rotary_embed(value_rows, token_positions):
    half_width = value_rows.shape[-1] // 2
    frequency = THETA ** (-(2.0 * jnp.arange(half_width, dtype=jnp.float32)) / value_rows.shape[-1])
    angle = token_positions.astype(jnp.float32)[:, None] * frequency[None, :]
    cosine = jnp.cos(angle)[None, :, None, :]
    sine = jnp.sin(angle)[None, :, None, :]
    first = value_rows[..., :half_width]
    second = value_rows[..., half_width:]
    return jnp.concatenate(
        [first * cosine - second * sine, second * cosine + first * sine], axis=-1
    )


def body(hidden, seq_len, target_rank, in_gain, joined_projection_weight, query_gain, k_gain):
    slots, length, width = hidden.shape
    ranks = lax.axis_size("dp")
    pair = -(-slots // ranks)
    lanes = ranks * pair
    local = jnp.arange(slots, dtype=jnp.int32)
    same_target = (target_rank[:, None] == target_rank[None, :]) & (local[None, :] < local[:, None])
    earlier = jnp.sum(same_target.astype(jnp.int32), axis=1)
    position = target_rank * pair + earlier
    lane_ids = jnp.arange(lanes, dtype=jnp.int32)
    hits = lane_ids[:, None] == position[None, :]
    filled = jnp.any(hits, axis=1)
    source = jnp.sum(jnp.where(hits, local[None, :], 0), axis=1)
    outgoing = jnp.where(
        filled[:, None, None], jnp.take(hidden, source, axis=0), jnp.zeros((), hidden.dtype)
    )
    sent_length = jnp.where(filled, jnp.take(seq_len, source), 0)
    arrived, arrived_length = (
        lax.all_to_all(
            outgoing.reshape(ranks, pair, length, width),
            "dp",
            split_axis=0,
            concat_axis=0,
            tiled=True,
        ),
        lax.all_to_all(
            sent_length.reshape(ranks, pair), "dp", split_axis=0, concat_axis=0, tiled=True
        ),
    )
    arrived = arrived.reshape(lanes, length, width)
    arrived_length = arrived_length.reshape(lanes)
    present = arrived_length > 0
    arrived_slot = jnp.cumsum(present.astype(jnp.int32)) - 1
    matches = (arrived_slot[None, :] == local[:, None]) & present[None, :]
    chosen = jnp.sum(jnp.where(matches, lane_ids[None, :], 0), axis=1)
    lengths = jnp.sum(jnp.where(matches, arrived_length[None, :], 0), axis=1)
    moved = arrived if lanes == slots else jnp.take(arrived, chosen, axis=0)
    whole = lax.all_gather(moved, ("tensor", "sub"), axis=2, tiled=True)
    tokens = whole.reshape(slots * length, whole.shape[2]).astype(jnp.float32)
    square_mean = jnp.mean(tokens * tokens, axis=-1, keepdims=True)
    normed_query = (tokens * lax.rsqrt(square_mean + EPS) * in_gain).astype(jnp.bfloat16)
    groups = joined_projection_weight.shape[1]
    head_dim = query_gain.shape[0]
    group_query = joined_projection_weight.shape[2] - 2 * head_dim
    half_heads = group_query // head_dim // lax.axis_size("sub")
    query_cols = half_heads * head_dim
    core = lax.axis_index("sub")
    own_query = lax.dynamic_slice_in_dim(joined_projection_weight, core * query_cols, query_cols, 2)
    extra = joined_projection_weight[:, :, group_query:]
    columns = jnp.concatenate([own_query, extra], axis=2)
    span = columns.shape[2]
    flat_columns = columns.reshape(columns.shape[0], groups * span)
    copies = lax.axis_size("groups")
    rows = flat_columns.shape[0] // copies
    own_rows = lax.dynamic_slice_in_dim(flat_columns, lax.axis_index("groups") * rows, rows, 0)
    mixed_projection = jnp.dot(
        normed_query,
        lax.all_gather(own_rows, ("dp", "groups"), axis=0, tiled=True),
        preferred_element_type=jnp.float32,
    )
    mixed_projection = mixed_projection.reshape(slots, length, groups, span)
    token_positions = jnp.arange(length, dtype=jnp.int32)
    live = token_positions[None, :] < lengths[:, None]
    query_rows = mixed_projection[..., :query_cols].reshape(
        slots, length, groups * half_heads, head_dim
    )
    query_rows = rotary_embed(per_head_norm(query_rows, query_gain), token_positions).astype(
        jnp.bfloat16
    )
    key_rows = rotary_embed(
        per_head_norm(mixed_projection[..., query_cols : query_cols + head_dim], k_gain),
        token_positions,
    )
    key_rows = jnp.where(live[:, :, None, None], key_rows, 0.0).astype(jnp.bfloat16)
    value_rows = jnp.where(
        live[:, :, None, None], mixed_projection[..., query_cols + head_dim :], 0.0
    ).astype(jnp.bfloat16)
    grouped_heads = query_rows.reshape(slots, length, groups, half_heads, head_dim)
    scores = jnp.einsum(
        "nqghd,nkgd->nghqk", grouped_heads, key_rows, preferred_element_type=jnp.float32
    ) * head_dim ** (-0.5)
    causal = token_positions[None, :] <= token_positions[:, None]
    allowed = causal[None, None, None, :, :] & live[:, None, None, None, :]
    weights = jnp.where(allowed, jnp.exp(scores), 0.0)
    probs = (weights / jnp.sum(weights, axis=-1, keepdims=True)).astype(jnp.bfloat16)
    context = jnp.einsum("nghqk,nkgd->nqghd", probs, value_rows, preferred_element_type=jnp.float32)
    context = jnp.where(live[:, :, None, None, None], context, 0.0)
    context = context.reshape(slots, length, groups, half_heads * head_dim).astype(jnp.bfloat16)
    share = length // lax.axis_size("sub")
    key_share = lax.dynamic_slice_in_dim(key_rows, core * share, share, 1).reshape(
        slots, share, groups * head_dim
    )
    value_share = lax.dynamic_slice_in_dim(value_rows, core * share, share, 1).reshape(
        slots, share, groups * head_dim
    )
    return (key_share, value_share, context)


CHUNK = 256


def exchange_kernel(
    tok, lens, w, q_out, kv_out, len_out,
    a, wm, psend, prec, own, ssend, srecv, scales, kvown, kvrecv, lrecv, relay,
    rs, rr, fs,
    s1s, s1r, s2s, s2r, s3s, s3r, s4s, s4r,
    ws, wr, wfs, wfr, ps, pr, ss, sr, ls, lr, kvs, kvr,
):
    g = lax.axis_index("groups")
    z = lax.axis_index("dp")
    x = lax.axis_index("tensor")
    s = lax.axis_index("sub")
    here = z % 2
    pair = z // 2
    half = w.shape[0] // 2
    n_chunks = wm.shape[0]
    x_mate = (g, z, 1 - x, s)
    sibling = (g, z, x, 1 - s)
    z_mate = (g, pair * 2 + (1 - here), x, s)
    y_mate = (1 - g, z, x, s)
    far = (g, (1 - pair) * 2 + here, x, s)

    barrier = pltpu.get_barrier_semaphore()
    for dz in range(1, 4):
        for dx in range(2):
            pl.semaphore_signal(
                barrier, inc=1, device_id=(g, (z + dz) % 4, (x + dx) % 2, s),
                device_id_type=pl.DeviceIdType.MESH,
            )
    for other in (x_mate, sibling, y_mate):
        pl.semaphore_signal(barrier, inc=1, device_id=other, device_id_type=pl.DeviceIdType.MESH)
    pl.semaphore_wait(barrier, 9)

    def remote(src, dst, send, recv, device):
        return pltpu.make_async_remote_copy(
            src_ref=src, dst_ref=dst, send_sem=send, recv_sem=recv,
            device_id=device, device_id_type=pl.DeviceIdType.MESH,
        )

    def first(o, b):
        target = 2 * ((x + 1 + o) % 2) + b
        zt = 2 * x + b
        near, across = tok.at[target, x], tok.at[target, 1 - x]
        return (
            zt == z,
            remote(near, a.at[o, s, z, x], s1s.at[o, b, 0], s1r.at[o, z], (g, zt, x, s)),
            pltpu.make_async_copy(near, a.at[o, s, z, x], s1r.at[o, z]),
            remote(across, a.at[o, s, z, 1 - x], s1s.at[o, b, 1], s1r.at[o, z], x_mate),
            remote(across, relay.at[o, b], rs.at[o, b], rr.at[o, b], x_mate),
        )

    def start_first(o):
        for b in range(2):
            stays, away, local, beside, over = first(o, b)
            pl.when(jnp.logical_not(stays))(over.start)
            pl.when(stays)(beside.start)
            pl.when(jnp.logical_not(stays))(away.start)
            pl.when(stays)(local.start)

    def onward(o, b):
        zt = 2 * (1 - x) + b
        return zt != z, remote(
            relay.at[o, b], a.at[o, s, z, x], fs.at[o, b], s1r.at[o, z], (g, zt, x, s)
        )

    def pass_on(o):
        for b in range(2):
            leaves, copy = onward(o, b)

            @pl.when(leaves)
            def _():
                remote(relay.at[o, b], relay.at[o, b], rs.at[o, b], rr.at[o, b], x_mate).wait_recv()
                copy.start()

    def arrived(o, zs):
        dst = a.at[o, s, zs, x]
        local = (pair == x) & (z == zs)
        pl.when(jnp.logical_not(local))(
            remote(dst, dst, s1s.at[o, 0, 0], s1r.at[o, zs], x_mate).wait_recv
        )
        pl.when(local)(pltpu.make_async_copy(tok.at[0, 0], dst, s1r.at[o, zs]).wait)

    def to_x(o, zs):
        piece = a.at[o, s, zs, x]
        return remote(piece, piece, s2s.at[o, zs], s2r.at[o, zs], x_mate)

    def from_x(o, zs):
        piece = a.at[o, s, zs, 1 - x]
        return remote(piece, piece, s2s.at[o, zs], s2r.at[o, zs], x_mate)

    def to_sub(o, zs):
        piece = a.at[o, s, zs, x]
        return remote(piece, piece, s3s.at[o, zs], s3r.at[o, zs], sibling)

    def from_sub(o, zs):
        piece = a.at[o, 1 - s, zs, x]
        return remote(piece, piece, s3s.at[o, zs], s3r.at[o, zs], sibling)

    def to_sub_late(o, zs):
        piece = a.at[o, s, zs, 1 - x]
        return remote(piece, piece, s4s.at[o, zs], s4r.at[o, zs], sibling)

    def from_sub_late(o, zs):
        piece = a.at[o, 1 - s, zs, 1 - x]
        return remote(piece, piece, s4s.at[o, zs], s4r.at[o, zs], sibling)

    def forward_first(o):
        for zs in range(4):
            arrived(o, zs)
            to_x(o, zs).start()
            to_sub(o, zs).start()

    def forward_second(o):
        for zs in range(4):
            from_x(o, zs).wait_recv()
            to_sub_late(o, zs).start()

    def forward_last(o):
        for zs in range(4):
            from_sub(o, zs).wait_recv()
            from_sub_late(o, zs).wait_recv()

    def w_copy(c):
        rows = pl.ds(pl.multiple_of(g * half, half), half)
        cols = pl.ds(pl.multiple_of(c * CHUNK, CHUNK), CHUNK)
        return remote(w.at[rows, cols], wm.at[c, rows], ws.at[c], wr.at[c], z_mate)

    def w_forward(c):
        rows = pl.ds(pl.multiple_of(g * half, half), half)
        return remote(wm.at[c, rows], wm.at[c, rows], wfs.at[c], wfr.at[c], y_mate)

    def w_forwarded(c):
        rows = pl.ds(pl.multiple_of((1 - g) * half, half), half)
        return remote(wm.at[c, rows], wm.at[c, rows], wfs.at[c], wfr.at[c], y_mate)

    def p_copy(c):
        return remote(psend.at[c], prec.at[c], ps.at[c], pr.at[c], far)

    def s_copy():
        return remote(ssend, srecv, ss.at[0], sr.at[0], far)

    def kv_copy():
        return remote(kvown, kvrecv, kvs.at[0], kvr.at[0], sibling)

    def len_copy(step):
        zt = (z + step) % 4
        return remote(lens.at[zt], lrecv.at[z], ls.at[step], lr.at[step], (g, zt, x, s))

    def product(o, c):
        def tokens(block):
            t = a[o, block]
            return t.reshape(t.shape[0] * t.shape[1] * t.shape[2], t.shape[3])

        cols = pl.ds(pl.multiple_of(c * CHUNK, CHUNK), CHUNK)
        return jnp.dot(
            tokens(here), w[:, cols], preferred_element_type=jnp.float32
        ) + jnp.dot(tokens(1 - here), wm[c], preferred_element_type=jnp.float32)

    def squares(o, zs):
        total = None
        for block in range(2):
            t = a[o, block, zs].reshape(128, a.shape[5]).astype(jnp.float32)
            part = jnp.sum(t * t, axis=1, keepdims=True)
            total = part if total is None else total + part
        return total

    start_first(0)
    for step in range(1, 4):
        len_copy(step).start()
    pass_on(0)
    for c in range(2):
        w_copy(c).start()

    forward_first(0)
    for c in range(2, n_chunks):
        w_copy(c).start()
    start_first(1)
    w_copy(0).wait_recv()
    w_forward(0).start()
    pass_on(1)
    forward_second(0)
    forward_last(0)

    def send_partial(c):
        w_forwarded(c).wait_recv()
        psend[c] = product(0, c).astype(psend.dtype)
        p_copy(c).start()

    @pl.loop(1, n_chunks)
    def _(c):
        w_copy(c).wait_recv()
        w_forward(c).start()
        send_partial(c - 1)
        pl.when(c == n_chunks - 2)(lambda: forward_first(1))
        pl.when(c == n_chunks - 1)(lambda: forward_second(1))

    send_partial(n_chunks - 1)

    @pl.loop(0, 4)
    def _(zs):
        ssend[zs] = jnp.broadcast_to(squares(0, zs), (128, 128)).T[:8]

    s_copy().start()

    forward_last(1)

    @pl.loop(0, n_chunks)
    def _(c):
        own[c] = product(1, c)

    s_copy().wait_recv()

    @pl.loop(0, 4)
    def _(zs):
        rows = pl.ds(pl.multiple_of(zs * 128, 128), 128)
        total = squares(1, zs) + jnp.broadcast_to(srecv[zs, 0:1], (128, 128)).T
        scales[rows, :] = lax.rsqrt(total / (4 * a.shape[5]) + EPS)

    scale = jnp.concatenate([scales[...]] * (CHUNK // 128), axis=1)
    p_copy(0).wait_recv()
    kvown[...] = (own[0] + prec[0].astype(jnp.float32)) * scale
    kv_copy().start()
    kv_out[s] = kvown[...]

    @pl.loop(1, n_chunks)
    def _(c):
        p_copy(c).wait_recv()
        wide = jnp.concatenate([scales[...]] * (CHUNK // 128), axis=1)
        q_out[c - 1] = (own[c] + prec[c].astype(jnp.float32)) * wide

    len_out[z] = lens[z]
    for step in range(1, 4):
        source = (z + 4 - step) % 4
        remote(lrecv.at[source], lrecv.at[source], ls.at[step], lr.at[step], x_mate).wait_recv()
        len_out[source] = lrecv[source]

    kv_copy().wait_recv()
    kv_out[1 - s] = kvrecv[...]

    for o in range(2):
        for b in range(2):
            stays, away, _, beside, over = first(o, b)
            pl.when(jnp.logical_not(stays))(over.wait_send)
            pl.when(stays)(beside.wait_send)
            pl.when(jnp.logical_not(stays))(away.wait_send)
            leaves, copy = onward(o, b)
            pl.when(leaves)(copy.wait_send)
        for zs in range(4):
            to_x(o, zs).wait_send()
            to_sub(o, zs).wait_send()
            to_sub_late(o, zs).wait_send()
    for c in range(n_chunks):
        w_copy(c).wait_send()
        w_forward(c).wait_send()
        p_copy(c).wait_send()
    s_copy().wait_send()
    kv_copy().wait_send()
    for step in range(1, 4):
        len_copy(step).wait_send()


def exchange(tok, lens, w):
    width = w.shape[0]
    columns = CHUNK
    chunks = w.shape[1] // columns
    tokens = tok.shape[0] * tok.shape[1] * tok.shape[2]
    dma = pltpu.SemaphoreType.DMA
    vmem = pl.BlockSpec(memory_space=pltpu.VMEM)
    f32 = jnp.float32
    bf16 = jnp.bfloat16
    return pl.pallas_call(
        exchange_kernel,
        out_shape=(
            jax.ShapeDtypeStruct((chunks - 1, tokens, columns), f32),
            jax.ShapeDtypeStruct((2, tokens, columns), f32),
            jax.ShapeDtypeStruct(lens.shape, f32),
        ),
        in_specs=[pl.BlockSpec(memory_space=pl.ANY), vmem, vmem],
        out_specs=(vmem, vmem, vmem),
        scratch_shapes=[
            pltpu.VMEM((2, 2, 4, 2, tok.shape[2], width), bf16),
            pltpu.VMEM((chunks, width, columns), bf16),
            pltpu.VMEM((chunks, tokens, columns), bf16),
            pltpu.VMEM((chunks, tokens, columns), bf16),
            pltpu.VMEM((chunks, tokens, columns), f32),
            pltpu.VMEM(lens.shape, f32),
            pltpu.VMEM(lens.shape, f32),
            pltpu.VMEM((tokens, 128), f32),
            pltpu.VMEM((tokens, columns), f32),
            pltpu.VMEM((tokens, columns), f32),
            pltpu.VMEM(lens.shape, f32),
            pltpu.VMEM((2, 2, tok.shape[2], width), bf16),
            dma((2, 2)), dma((2, 2)), dma((2, 2)),
            dma((2, 2, 2)), dma((2, 4)), dma((2, 4)), dma((2, 4)),
            dma((2, 4)), dma((2, 4)), dma((2, 4)), dma((2, 4)),
            dma((chunks,)), dma((chunks,)), dma((chunks,)), dma((chunks,)),
            dma((chunks,)), dma((chunks,)), dma((1,)), dma((1,)),
            dma((4,)), dma((4,)), dma((1,)), dma((1,)),
        ],
        compiler_params=pltpu.CompilerParams(
            collective_id=0, has_side_effects=True, vmem_limit_bytes=48 << 20
        ),
        cost_estimate=pl.CostEstimate(
            flops=8 * tokens * width * chunks * columns, bytes_accessed=1 << 24, transcendentals=0
        ),
        name="exchange",
    )(tok, lens, w)


def attend_kernel(q_ref, kv_ref, len_ref, cos_ref, sin_ref, qg_ref, kg_ref, k_out, v_out, ctx_out):
    head = cos_ref.shape[1]
    rows = cos_ref.shape[0]
    seqs, share, _ = k_out.shape
    length = rows // seqs
    core = lax.axis_index("sub")
    len_key = jnp.broadcast_to(len_ref[0, 0:1, :], (rows, rows))
    len_query = len_key.T
    row_ids = lax.broadcasted_iota(jnp.int32, (rows, rows), 0)
    col_ids = lax.broadcasted_iota(jnp.int32, (rows, rows), 1)
    key_pos = (col_ids % length).astype(jnp.float32)
    query_pos = (row_ids % length).astype(jnp.float32)
    allowed = (
        (row_ids // length == col_ids // length) & (col_ids <= row_ids) & (key_pos < len_key)
    )
    live = query_pos < len_query
    cos = cos_ref[...]
    sin = sin_ref[...]

    def norm_rope(t, gain):
        mean = jnp.mean(t * t, axis=-1, keepdims=True)
        t = t * lax.rsqrt(mean + EPS) * gain
        return t * cos + pltpu.roll(t, head // 2, 1) * sin

    def part(t):
        t = t.reshape(seqs, length, head)
        return jnp.where(core == 0, t[:, :share], t[:, share:])

    kgain = kg_ref[...]
    qgain = qg_ref[...]
    n_groups = kv_ref.shape[2] // head
    heads = q_ref.shape[0] * q_ref.shape[2] // head // n_groups
    per_chunk = q_ref.shape[2] // head
    for group in range(n_groups):
        cols = slice(group * head, (group + 1) * head)
        key = jnp.where(live, norm_rope(kv_ref[0, :, cols], kgain), 0.0)
        value = jnp.where(live, kv_ref[1, :, cols], 0.0)
        k_out[:, :, cols] = part(key).astype(k_out.dtype)
        v_out[:, :, cols] = part(value).astype(v_out.dtype)
        key = key.astype(jnp.bfloat16)
        value = value.astype(jnp.bfloat16)
        for h in range(heads):
            n = group * heads + h
            at = n % per_chunk * head
            query = norm_rope(q_ref[n // per_chunk, :, at : at + head], qgain)
            scores = lax.dot_general(
                query.astype(jnp.bfloat16), key, (((1,), (1,)), ((), ())),
                preferred_element_type=jnp.float32,
            ) * head ** (-0.5)
            weights = jnp.where(allowed, jnp.exp(scores), 0.0)
            probs = weights / jnp.sum(weights, axis=-1, keepdims=True)
            out = jnp.dot(probs.astype(jnp.bfloat16), value, preferred_element_type=jnp.float32)
            ctx_out[:, n * head : (n + 1) * head] = jnp.where(live, out, 0.0).astype(ctx_out.dtype)


def attend(q, kv, lens, query_gain, k_gain, length, share):
    head = query_gain.shape[0]
    chunks, tokens, columns = q.shape
    blocks = lens.shape[0]
    rows = tokens // blocks
    seqs = rows // length
    frequency = THETA ** (-(2.0 * jnp.arange(head // 2, dtype=jnp.float32)) / head)
    positions = jnp.arange(rows, dtype=jnp.int32) % length
    angle = positions.astype(jnp.float32)[:, None] * frequency[None, :]
    cos = jnp.cos(angle)
    sin = jnp.sin(angle)
    whole = lambda *shape: pl.BlockSpec(shape, lambda i: (0,) * len(shape))
    cache = jax.ShapeDtypeStruct((tokens // length, share, columns), jnp.bfloat16)
    return pl.pallas_call(
        attend_kernel,
        grid=(blocks,),
        out_shape=(cache, cache, jax.ShapeDtypeStruct((tokens, chunks * columns), jnp.bfloat16)),
        in_specs=[
            pl.BlockSpec((chunks, rows, columns), lambda i: (0, i, 0)),
            pl.BlockSpec((2, rows, columns), lambda i: (0, i, 0)),
            pl.BlockSpec((1,) + lens.shape[1:], lambda i: (i, 0, 0)),
            whole(rows, head), whole(rows, head), whole(1, head), whole(1, head),
        ],
        out_specs=(
            pl.BlockSpec((seqs, share, columns), lambda i: (i, 0, 0)),
            pl.BlockSpec((seqs, share, columns), lambda i: (i, 0, 0)),
            pl.BlockSpec((rows, chunks * columns), lambda i: (i, 0)),
        ),
        compiler_params=pltpu.CompilerParams(vmem_limit_bytes=32 << 20),
        name="attend",
    )(
        q, kv, lens,
        jnp.concatenate([cos, cos], axis=1), jnp.concatenate([-sin, sin], axis=1),
        query_gain[None, :], k_gain[None, :],
    )


def paired_body(
    hidden, seq_len, target_rank, in_gain, joined_projection_weight, query_gain, k_gain
):
    slots, length, width = hidden.shape
    ranks = lax.axis_size("dp")
    pair = slots // ranks
    local = jnp.arange(slots, dtype=jnp.int32)
    same_target = (target_rank[:, None] == target_rank[None, :]) & (local[None, :] < local[:, None])
    position = target_rank * pair + jnp.sum(same_target.astype(jnp.int32), axis=1)
    hits = local[:, None] == position[None, :]
    source = jnp.sum(jnp.where(hits, local[None, :], 0), axis=1)
    sent_length = jnp.sum(jnp.where(hits, seq_len[None, :], 0), axis=1)
    tok = jnp.take(hidden, source, axis=0, mode="clip").reshape(ranks, 2, pair // 2 * length, width)
    lens = jnp.broadcast_to(
        sent_length.astype(jnp.float32).reshape(ranks, 1, pair, 1), (ranks, 8, pair, length)
    ).reshape(ranks, 8, pair * length)

    head = query_gain.shape[0]
    rows, groups, span = joined_projection_weight.shape
    group_query = span - 2 * head
    query_cols = group_query // lax.axis_size("sub")
    core = lax.axis_index("sub")
    gain = lax.dynamic_slice_in_dim(in_gain, lax.axis_index("dp") * rows, rows, 0)
    own_query = lax.dynamic_slice_in_dim(joined_projection_weight, core * query_cols, query_cols, 2)
    own_kv = lax.dynamic_slice_in_dim(
        joined_projection_weight, group_query + core * head, head, 2
    )
    columns = [own_kv[:, i] for i in range(groups)] + [own_query[:, i] for i in range(groups)]
    flat = jnp.concatenate(columns, axis=1).astype(jnp.float32) * gain[:, None]
    w = flat.astype(jnp.bfloat16)

    q, kv, lengths = exchange(tok, lens, w)
    share = length // lax.axis_size("sub")
    key_share, value_share, context = attend(q, kv, lengths, query_gain, k_gain, length, share)
    return (key_share, value_share, context.reshape(slots, length, groups, query_cols))


def solution(mesh):
    sizes = mesh.shape
    paired = (
        sizes["dp"] == 4 and sizes["tensor"] == 2 and sizes["sub"] == 2 and sizes["groups"] == 2
    )
    placed = (
        P(("groups", "dp"), None, ("tensor", "sub")),
        P(("groups", "dp")),
        P(("groups", "dp")),
        P(),
        P("dp", "tensor", None),
        P(),
        P(),
    )
    return jax.shard_map(
        paired_body if paired else body,
        mesh=mesh,
        in_specs=placed,
        out_specs=(
            P(("groups", "dp"), "sub", "tensor"),
            P(("groups", "dp"), "sub", "tensor"),
            P(("groups", "dp"), None, "tensor", "sub"),
        ),
        check_vma=False,
    )
```
